512 devices in a mesh: replica: 16 (over y_lo, x, core), fsdp: 32 (over z, y_hi).
Axes of the slice: x: 4, y: 8 (y_hi: 4, y_lo: 2; y = y_hi * 2 + y_lo), z: 8, core: 2. Of those that a mesh axis runs over, the one named last changes fastest.
Arguments:
- activations: bfloat16 [16, 4096, 8192], P('replica', 'fsdp'), may hold values from -30 to 30, as said below
- key_cotangent: bfloat16 [16, 4096, 512], P('replica', 'fsdp'), may hold values from -6 to 6
- key_gain: float32 [128], replicated, may hold values from 0.25 to 1.75
- local_weight: float32 [16, 8192, 512], P('replica', 'fsdp'), may hold values from -6 to 6
- global_weight: float32 [8192, 512], P('fsdp', 'replica'), may hold values from -6 to 6
- outer_momentum: float32 [8192, 512], P('fsdp', 'replica'), may hold values from -6 to 6
- late_delta: float32 [8192, 512], P('fsdp', 'replica'), may hold values from -6 to 6
Outputs:
- next_local: float32 [16, 8192, 512], P('replica', 'fsdp')
- next_global: float32 [8192, 512], P('fsdp', 'replica')
- next_momentum: float32 [8192, 512], P('fsdp', 'replica')
- outer_delta: float32 [8192, 512], P('fsdp', 'replica')
The draws below stay inside these ranges and needn't reach their ends.
Inputs may be any that keep to these rules, and one draw needn't show every extreme that they name: The activations are the key projection's normalized inputs, and the scale of each input feature differs from feature to feature (by up to about twentyfold).
All inputs are finite; a program needn't handle non-finite values.
Results may differ from the reference program's by a relative error of at most 0.00083.
Values may be sent and summed in bfloat16 or wider, within the bound.
No kernel may reach another device: no remote copies, remote signals or barrier semaphores. Data moves between devices by JAX's collectives and lax.ppermute only.
A program may use at most 64 MiB of HBM per device.

```python
import jax
import jax.numpy as jnp
from jax import lax

D = 8192
HEAD = 128
C = 512
TOKENS = 4096
REPLICAS = 16


def draw_activations(key, part):
    key = jax.random.fold_in(key, 11)
    first, second = jax.random.split(key, 2)
    place = jnp.arange(D, dtype=jnp.float32) / (D - 1)
    column = 0.3 * 10.0 ** place * jnp.exp(jax.random.uniform(second, (D,), jnp.float32, -0.4, 0.4))
    base = jax.random.normal(first, (REPLICAS, TOKENS, D), jnp.float32)
    return (jnp.clip(base, -6.0, 6.0) * column).astype(jnp.bfloat16)


def raised(result, own_key, source, target, shards_of, factor):
    def block_of(dim):
        return (jnp.arange(result.shape[dim]) // (result.shape[dim] // shards_of)).reshape((-1,) + (1,) * (result.ndim - 1 - dim))

    first = jax.random.permutation(own_key, shards_of)[block_of(target)]
    far = (block_of(target) + shards_of // 2) % shards_of
    return jnp.where((block_of(source) == first) | (block_of(source) == far), factor * result, result)


def level_of(stream_key, shape, cuts, smallest, high):
    level, own = 1.0, jax.random.fold_in(stream_key, 6)
    for position, shards_of in cuts:
        steps = jnp.exp(jax.random.uniform(jax.random.fold_in(own, position), (shards_of,), jnp.float32, smallest / len(cuts), high / len(cuts)))
        level = level * jnp.repeat(steps, shape[position] // shards_of).reshape([-1 if axis == position else 1 for axis in range(len(shape))])
    return level


def noise(own_key, extent, scale, bound, cuts=(), kind=jnp.bfloat16):
    drawn = scale * jax.random.normal(own_key, extent, jnp.float32)
    if cuts:
        drawn = drawn * level_of(own_key, extent, cuts, -0.22, 0.18)
    return jnp.clip(drawn, -bound, bound).astype(kind)


def heavy_noise(stream_key, dims, scale, limit, pieces, heavy, kind=jnp.bfloat16):
    values = scale * jax.random.normal(stream_key, dims, jnp.float32)
    if pieces:
        values = values * level_of(stream_key, dims, pieces, -0.22, 0.18)
    return jnp.clip(raised(values, jax.random.fold_in(stream_key, 3), *heavy), -limit, limit).astype(kind)


def setup_inputs(seed: int = 0) -> dict:
    seeds = jax.random.split(jax.random.key(seed), 8)
    return {
        "activations": draw_activations(jax.random.fold_in(seeds[7], 71), 0),
        "key_cotangent": noise(seeds[1], (REPLICAS, TOKENS, C), 1.0, 6.0, ((0, 16), (1, 32))),
        "key_gain": jnp.clip(1.0 + 0.15 * jax.random.normal(seeds[2], (HEAD,), jnp.float32), 0.25, 1.75),
        "local_weight": heavy_noise(seeds[3], (REPLICAS, D, C), 1.0, 6.0, ((0, 16), (1, 32)), (0, 2, 16, 2.0), jnp.float32),
        "global_weight": noise(seeds[4], (D, C), 1.0, 6.0, ((0, 32), (1, 16)), jnp.float32),
        "outer_momentum": noise(seeds[5], (D, C), 0.5, 6.0, ((0, 32), (1, 16)), jnp.float32),
        "late_delta": noise(seeds[6], (D, C), 0.5, 6.0, ((0, 32), (1, 16)), jnp.float32),
    }


inner_rate = 0.5
outer_rate = 0.7
keep_rate = 0.9
blend_rate = 0.5
epsilon = 1e-06

def step_replica(feats, cotangent, weight, gain):
    width = feats.shape[1]
    factor = width ** (-0.5)
    hidden = jnp.dot(feats, weight.astype(jnp.bfloat16), preferred_element_type=jnp.float32) * factor
    tokens = hidden.shape[0]
    shaped = hidden.reshape(tokens, -1, HEAD)
    spread = jnp.sqrt(lax.optimization_barrier(jnp.mean(shaped * shaped, axis=-1, keepdims=True)) + epsilon)
    unit = shaped / spread
    slope = cotangent.astype(jnp.float32).reshape(tokens, -1, HEAD) * gain
    key_slope = (slope - unit * lax.optimization_barrier(jnp.mean(slope * unit, axis=-1, keepdims=True))) / spread
    key_slope = key_slope.reshape(tokens, -1).astype(jnp.bfloat16)
    gradient = jnp.dot(feats.T, key_slope, preferred_element_type=jnp.float32) * factor
    grad_scale = jnp.sqrt(jnp.sum(gradient * gradient) / gradient.size + epsilon)
    return weight - inner_rate * gradient / grad_scale

def reference(activations, key_cotangent, key_gain, local_weight, global_weight, outer_momentum, late_delta):
    after_step = lax.map(lambda items: step_replica(items[0], items[1], items[2], key_gain), (activations, key_cotangent, local_weight))
    outer_delta = lax.optimization_barrier(jnp.sum(global_weight[None] - after_step, axis=0)) / REPLICAS
    next_momentum = keep_rate * outer_momentum + late_delta
    next_global = global_weight - outer_rate * (late_delta + keep_rate * next_momentum)
    next_local = blend_rate * next_global[None] + (1.0 - blend_rate) * after_step
    return (next_local, next_global, next_momentum, outer_delta)
```

```python
import functools

import jax
import jax.numpy as jnp
from jax import lax
from jax.experimental import pallas as pl
from jax.experimental.pallas import tpu as pltpu
from jax.sharding import Mesh
from jax.sharding import PartitionSpec as P

HEAD = 128

inner_rate = 0.5
outer_rate = 0.7
keep_rate = 0.9
blend_rate = 0.5
epsilon = 1e-06

REPLICA = ("y_lo", "x", "core")
FSDP = ("z", "y_hi")


def slope_kernel(factor, parts_ref, cotangent_ref, gain_ref, out_ref):
    pieces = parts_ref.shape[0]
    gain = gain_ref[...]
    for head in range(out_ref.shape[2] // HEAD):
        lanes = slice(head * HEAD, (head + 1) * HEAD)
        hidden = parts_ref[0, :, lanes].astype(jnp.float32)
        for piece in range(1, pieces):
            hidden = hidden + parts_ref[piece, :, lanes].astype(jnp.float32)
        hidden = hidden * factor
        spread = jnp.sqrt(jnp.mean(hidden * hidden, axis=-1, keepdims=True) + epsilon)
        unit = hidden / spread
        slope = cotangent_ref[:, lanes].astype(jnp.float32) * gain
        key_slope = (slope - unit * jnp.mean(slope * unit, axis=-1, keepdims=True)) / spread
        key_slope = key_slope.astype(jnp.bfloat16)
        for piece in range(out_ref.shape[0]):
            out_ref[piece, :, lanes] = key_slope


def key_slopes(parts, cotangent, gain, factor):
    return pl.pallas_call(
        functools.partial(slope_kernel, factor),
        out_shape=jax.ShapeDtypeStruct(parts.shape, jnp.bfloat16),
        compiler_params=pltpu.CompilerParams(vmem_limit_bytes=16 * 1024 * 1024),
        cost_estimate=pl.CostEstimate(flops=2_000_000, bytes_accessed=2_500_000, transcendentals=2000),
    )(parts, cotangent, gain)


def split_kernel(feats_ref, out_ref, sems):
    pieces, _, width = out_ref.shape
    copies = [
        pltpu.make_async_copy(feats_ref.at[:, pl.ds(i * width, width)], out_ref.at[i], sems.at[i])
        for i in range(pieces)
    ]
    for copy in copies:
        copy.start()
    for copy in copies:
        copy.wait()


def split_columns(feats, pieces):
    tokens, width = feats.shape
    return pl.pallas_call(
        split_kernel,
        out_shape=jax.ShapeDtypeStruct((pieces, tokens, width // pieces), feats.dtype),
        in_specs=[pl.BlockSpec(memory_space=pl.ANY)],
        out_specs=pl.BlockSpec(memory_space=pl.ANY),
        scratch_shapes=[pltpu.SemaphoreType.DMA((pieces,))],
        compiler_params=pltpu.CompilerParams(vmem_limit_bytes=16 * 1024 * 1024),
        cost_estimate=pl.CostEstimate(flops=0, bytes_accessed=4 * tokens * width, transcendentals=0),
    )(feats)


def gather_by_permutes(x, axis):
    size = lax.axis_size(axis)
    me = lax.axis_index(axis)
    out = jnp.zeros((size,) + x.shape, x.dtype)
    for step in range(size):
        piece = x
        if step:
            piece = lax.ppermute(x, axis, [(i, (i + step) % size) for i in range(size)])
        out = lax.dynamic_update_index_in_dim(out, piece, lax.rem(me + size - step, size), 0)
    return out


def shards(
    activations, key_cotangent, key_gain, local_weight, global_weight, outer_momentum, late_delta
):
    feats = activations[0]
    own_rows = local_weight[0]
    tokens, width = feats.shape
    rows, columns = own_rows.shape
    factor = width ** (-0.5)
    z_size = lax.axis_size("z")
    y_size = lax.axis_size("y_hi")
    replicas = lax.axis_size(REPLICA)

    owned = lax.all_to_all(split_columns(feats, z_size), "z", 0, 0)
    owned = owned.reshape(z_size * tokens, width // z_size)

    weight = gather_by_permutes(own_rows.astype(jnp.bfloat16), "y_hi").reshape(-1, columns)
    global_t, momentum_t, late_t = global_weight.T, outer_momentum.T, late_delta.T
    next_momentum_t = keep_rate * momentum_t + late_t
    next_global_t = global_t - outer_rate * (late_t + keep_rate * next_momentum_t)
    new_rows_t = gather_by_permutes(next_global_t, "core")
    new_rows_t = gather_by_permutes(new_rows_t, "y_lo")
    new_rows_t = gather_by_permutes(new_rows_t, "x")
    new_rows = new_rows_t.transpose(1, 0, 2, 3, 4).reshape(columns, rows).T

    partial_hidden = jnp.dot(owned, weight, preferred_element_type=jnp.float32).astype(jnp.bfloat16)
    parts = lax.all_to_all(partial_hidden.reshape(z_size, tokens, columns), "z", 0, 0)
    slopes = key_slopes(parts, key_cotangent[0], key_gain.reshape(1, HEAD), factor)
    slopes = lax.all_to_all(slopes, "z", 0, 0).reshape(z_size * tokens, columns)

    bound = 30.0 * slopes.shape[0] * jnp.max(jnp.abs(slopes)).astype(jnp.float32)
    exponent = jnp.ceil(jnp.log2(jnp.maximum(bound, 1e-30))) - 15.0
    scaled = lax.dot_general(
        owned, slopes, (((0,), (0,)), ((), ())), preferred_element_type=jnp.float32
    ) * jnp.exp2(-exponent)
    scaled = scaled.astype(jnp.float16).reshape(y_size, rows, columns)
    marks = jnp.full((y_size, 16, columns), exponent, jnp.float32).astype(jnp.float16)
    pieces = lax.all_to_all(jnp.concatenate([scaled, marks], axis=1), "y_hi", 0, 0)
    unscale = jnp.exp2(pieces[:, rows, 0].astype(jnp.float32)) * factor
    gradient = jnp.sum(pieces[:, :rows].astype(jnp.float32) * unscale[:, None, None], axis=0)

    squares = jnp.sum(gradient * gradient)
    shares = lax.all_to_all(jnp.broadcast_to(squares, (z_size * y_size, 1, 128)), FSDP, 0, 0)
    squares = jnp.sum(shares[:, 0, 0])
    grad_scale = jnp.sqrt(squares / (width * columns) + epsilon)
    after_step = own_rows - inner_rate * gradient / grad_scale

    sent_rows = after_step.T.reshape(replicas, columns // replicas, rows)
    received = lax.all_to_all(sent_rows, REPLICA, 0, 0)
    outer_delta_t = global_t - jnp.sum(received, axis=0) / replicas
    next_local = blend_rate * new_rows + (1.0 - blend_rate) * after_step
    return (next_local[None], next_global_t.T, next_momentum_t.T, outer_delta_t.T)


def solution(mesh):
    split = Mesh(mesh.devices.reshape(2, 4, 2, 8, 4), ("y_lo", "x", "core", "z", "y_hi"))
    whole = P(REPLICA, FSDP, None)
    outer = P(FSDP, REPLICA)
    return jax.shard_map(
        shards,
        mesh=split,
        in_specs=(whole, whole, P(), whole, outer, outer, outer),
        out_specs=(whole, outer, outer, outer),
        check_vma=False,
    )
```

```python
import functools

import jax
import jax.numpy as jnp
from jax import lax
from jax.experimental import pallas as pl
from jax.experimental.pallas import tpu as pltpu
from jax.sharding import Mesh
from jax.sharding import PartitionSpec as P

HEAD = 128

inner_rate = 0.5
outer_rate = 0.7
keep_rate = 0.9
blend_rate = 0.5
epsilon = 1e-06

REPLICA = ("y_lo", "x", "core")
FSDP = ("z", "y_hi")


def slope_kernel(factor, parts_ref, cotangent_ref, gain_ref, out_ref):
    pieces = parts_ref.shape[0]
    gain = gain_ref[...]
    for head in range(out_ref.shape[2] // HEAD):
        lanes = slice(head * HEAD, (head + 1) * HEAD)
        hidden = parts_ref[0, :, lanes].astype(jnp.float32)
        for piece in range(1, pieces):
            hidden = hidden + parts_ref[piece, :, lanes].astype(jnp.float32)
        hidden = hidden * factor
        spread = jnp.sqrt(jnp.mean(hidden * hidden, axis=-1, keepdims=True) + epsilon)
        unit = hidden / spread
        slope = cotangent_ref[:, lanes].astype(jnp.float32) * gain
        key_slope = (slope - unit * jnp.mean(slope * unit, axis=-1, keepdims=True)) / spread
        key_slope = key_slope.astype(jnp.bfloat16)
        for piece in range(out_ref.shape[0]):
            out_ref[piece, :, lanes] = key_slope


def key_slopes(parts, cotangent, gain, factor):
    return pl.pallas_call(
        functools.partial(slope_kernel, factor),
        out_shape=jax.ShapeDtypeStruct(parts.shape, jnp.bfloat16),
        compiler_params=pltpu.CompilerParams(vmem_limit_bytes=16 * 1024 * 1024),
        cost_estimate=pl.CostEstimate(flops=2_000_000, bytes_accessed=2_500_000, transcendentals=2000),
    )(parts, cotangent, gain)


def split_kernel(feats_ref, out_ref, sems):
    pieces, _, width = out_ref.shape
    copies = [
        pltpu.make_async_copy(feats_ref.at[:, pl.ds(i * width, width)], out_ref.at[i], sems.at[i])
        for i in range(pieces)
    ]
    for copy in copies:
        copy.start()
    for copy in copies:
        copy.wait()


def split_columns(feats, pieces):
    tokens, width = feats.shape
    return pl.pallas_call(
        split_kernel,
        out_shape=jax.ShapeDtypeStruct((pieces, tokens, width // pieces), feats.dtype),
        in_specs=[pl.BlockSpec(memory_space=pl.ANY)],
        out_specs=pl.BlockSpec(memory_space=pl.ANY),
        scratch_shapes=[pltpu.SemaphoreType.DMA((pieces,))],
        compiler_params=pltpu.CompilerParams(vmem_limit_bytes=16 * 1024 * 1024),
        cost_estimate=pl.CostEstimate(flops=0, bytes_accessed=4 * tokens * width, transcendentals=0),
    )(feats)


def gather_by_permutes(x, axis):
    size = lax.axis_size(axis)
    me = lax.axis_index(axis)
    out = jnp.zeros((size,) + x.shape, x.dtype)
    for step in range(size):
        piece = x
        if step:
            piece = lax.ppermute(x, axis, [(i, (i + step) % size) for i in range(size)])
        out = lax.dynamic_update_index_in_dim(out, piece, lax.rem(me + size - step, size), 0)
    return out


def project_kernel(owned_ref, weight_ref, out_ref):
    out_ref[...] = jnp.dot(
        owned_ref[...], weight_ref[...], preferred_element_type=jnp.float32
    ).astype(out_ref.dtype)


def project(owned, weight):
    rows, depth = owned.shape
    columns = weight.shape[1]
    block = rows // 4
    return pl.pallas_call(
        project_kernel,
        grid=(rows // block,),
        out_shape=jax.ShapeDtypeStruct((rows, columns), jnp.bfloat16),
        in_specs=[
            pl.BlockSpec((block, depth), lambda i: (i, 0)),
            pl.BlockSpec((depth, columns), lambda i: (0, 0)),
        ],
        out_specs=pl.BlockSpec((block, columns), lambda i: (i, 0)),
        compiler_params=pltpu.CompilerParams(vmem_limit_bytes=24 * 1024 * 1024),
        cost_estimate=pl.CostEstimate(
            flops=2 * rows * depth * columns,
            bytes_accessed=2 * (rows * depth + depth * columns + rows * columns),
            transcendentals=0,
        ),
    )(owned, weight)


MARKS = 16


def gradient_kernel(owned_ref, slopes_ref, out_ref, exponent_ref):
    @pl.when(pl.program_id(0) == 0)
    def _():
        largest = jnp.max(jnp.abs(slopes_ref[...]).astype(jnp.float32), axis=0, keepdims=True)
        bound = 30.0 * slopes_ref.shape[0] * jnp.max(largest, axis=1, keepdims=True)
        exponent = jnp.ceil(jnp.log2(jnp.maximum(bound, 1e-30))) - 15.0
        exponent_ref[...] = jnp.broadcast_to(exponent, exponent_ref.shape)

    rows = out_ref.shape[1] - MARKS
    sums = lax.dot_general(
        owned_ref[...], slopes_ref[...], (((0,), (0,)), ((), ())), preferred_element_type=jnp.float32
    )
    out_ref[0, :rows] = sums * jnp.exp2(-exponent_ref[0:1, 0:1])
    out_ref[0, rows:] = jnp.broadcast_to(exponent_ref[0:1, 0:1], (MARKS, out_ref.shape[2]))


def gradient_parts(owned, slopes, pieces):
    tokens, width = owned.shape
    columns = slopes.shape[1]
    rows = width // pieces
    return pl.pallas_call(
        gradient_kernel,
        grid=(pieces,),
        out_shape=jax.ShapeDtypeStruct((pieces, rows + MARKS, columns), jnp.float32),
        in_specs=[
            pl.BlockSpec((tokens, rows), lambda i: (0, i)),
            pl.BlockSpec((tokens, columns), lambda i: (0, 0)),
        ],
        out_specs=pl.BlockSpec((1, rows + MARKS, columns), lambda i: (i, 0, 0)),
        scratch_shapes=[pltpu.VMEM((8, 128), jnp.float32)],
        compiler_params=pltpu.CompilerParams(vmem_limit_bytes=24 * 1024 * 1024),
        cost_estimate=pl.CostEstimate(
            flops=2 * tokens * width * columns,
            bytes_accessed=2 * (tokens * width + tokens * columns) + 4 * width * columns,
            transcendentals=0,
        ),
    )(owned, slopes)


def shards(
    activations, key_cotangent, key_gain, local_weight, global_weight, outer_momentum, late_delta
):
    feats = activations[0]
    own_rows = local_weight[0]
    tokens, width = feats.shape
    rows, columns = own_rows.shape
    factor = width ** (-0.5)
    z_size = lax.axis_size("z")
    y_size = lax.axis_size("y_hi")
    replicas = lax.axis_size(REPLICA)

    owned = lax.all_to_all(split_columns(feats, z_size), "z", 0, 0)
    owned = owned.reshape(z_size * tokens, width // z_size)

    weight = gather_by_permutes(own_rows.astype(jnp.bfloat16), "y_hi").reshape(-1, columns)
    global_t, momentum_t, late_t = global_weight.T, outer_momentum.T, late_delta.T
    next_momentum_t = keep_rate * momentum_t + late_t
    next_global_t = global_t - outer_rate * (late_t + keep_rate * next_momentum_t)
    new_rows_t = gather_by_permutes(next_global_t, "core")
    new_rows_t = gather_by_permutes(new_rows_t, "y_lo")
    new_rows_t = gather_by_permutes(new_rows_t, "x")
    new_rows = new_rows_t.transpose(1, 0, 2, 3, 4).reshape(columns, rows).T

    owned, weight, new_rows = lax.optimization_barrier((owned, weight, new_rows))
    parts = project(owned, weight).reshape(z_size, tokens, columns)
    parts = lax.all_to_all(parts, "z", 0, 0)
    slopes = key_slopes(parts, key_cotangent[0], key_gain.reshape(1, HEAD), factor)
    slopes = lax.all_to_all(slopes, "z", 0, 0).reshape(z_size * tokens, columns)

    scaled = gradient_parts(owned, slopes, y_size).astype(jnp.float16)
    pieces = lax.all_to_all(scaled, "y_hi", 0, 0)
    unscale = jnp.exp2(pieces[:, rows, 0].astype(jnp.float32)) * factor
    gradient = jnp.sum(pieces[:, :rows].astype(jnp.float32) * unscale[:, None, None], axis=0)

    squares = jnp.sum(gradient * gradient)
    shares = lax.all_to_all(jnp.broadcast_to(squares, (z_size * y_size, 1, 128)), FSDP, 0, 0)
    squares = jnp.sum(shares[:, 0, 0])
    grad_scale = jnp.sqrt(squares / (width * columns) + epsilon)
    after_step = own_rows - inner_rate * gradient / grad_scale

    sent_rows = after_step.T.reshape(replicas, columns // replicas, rows).astype(jnp.float16)
    received = lax.all_to_all(sent_rows, REPLICA, 0, 0).astype(jnp.float32)
    outer_delta_t = global_t - jnp.sum(received, axis=0) / replicas
    next_local = blend_rate * new_rows + (1.0 - blend_rate) * after_step
    return (next_local[None], next_global_t.T, next_momentum_t.T, outer_delta_t.T)


def solution(mesh):
    split = Mesh(mesh.devices.reshape(2, 4, 2, 8, 4), ("y_lo", "x", "core", "z", "y_hi"))
    whole = P(REPLICA, FSDP, None)
    outer = P(FSDP, REPLICA)
    return jax.shard_map(
        shards,
        mesh=split,
        in_specs=(whole, whole, P(), whole, outer, outer, outer),
        out_specs=(whole, outer, outer, outer),
        check_vma=False,
    )
```

```python
import functools

import jax
import jax.numpy as jnp
from jax import lax
from jax.experimental import pallas as pl
from jax.experimental.pallas import tpu as pltpu
from jax.sharding import Mesh
from jax.sharding import PartitionSpec as P

HEAD = 128

inner_rate = 0.5
outer_rate = 0.7
keep_rate = 0.9
blend_rate = 0.5
epsilon = 1e-06

REPLICA = ("y_lo", "x", "core")
FSDP = ("z", "y_hi")
ALL = REPLICA + FSDP

EIGHT, FOUR = 8, 4


def place(core, p, q):
    return (p, q) if core == 0 else (2 * q + p // 4, p % 4)


def device(y_lo, x, core, p, q):
    z, y_hi = place(core, p, q)
    return (((y_lo * 4 + x) * 2 + core) * 8 + z) * 4 + y_hi


TEAMS = [(y_lo, x, core) for y_lo in range(2) for x in range(4) for core in range(2)]
RINGS_OF_8 = [[device(*team, p, q) for p in range(EIGHT)] for team in TEAMS for q in range(FOUR)]
RINGS_OF_4 = [[device(*team, p, q) for q in range(FOUR)] for team in TEAMS for p in range(EIGHT)]


def slope_kernel(factor, parts_ref, cotangent_ref, gain_ref, out_ref):
    pieces = parts_ref.shape[0]
    gain = gain_ref[...]
    for head in range(out_ref.shape[2] // HEAD):
        lanes = slice(head * HEAD, (head + 1) * HEAD)
        hidden = parts_ref[0, :, lanes].astype(jnp.float32)
        for piece in range(1, pieces):
            hidden = hidden + parts_ref[piece, :, lanes].astype(jnp.float32)
        hidden = hidden * factor
        spread = jnp.sqrt(jnp.mean(hidden * hidden, axis=-1, keepdims=True) + epsilon)
        unit = hidden / spread
        slope = cotangent_ref[:, lanes].astype(jnp.float32) * gain
        key_slope = (slope - unit * jnp.mean(slope * unit, axis=-1, keepdims=True)) / spread
        key_slope = key_slope.astype(jnp.bfloat16)
        for piece in range(out_ref.shape[0]):
            out_ref[piece, :, lanes] = key_slope


def key_slopes(parts, cotangent, gain, factor):
    return pl.pallas_call(
        functools.partial(slope_kernel, factor),
        out_shape=jax.ShapeDtypeStruct(parts.shape, jnp.bfloat16),
        compiler_params=pltpu.CompilerParams(vmem_limit_bytes=16 * 1024 * 1024),
        cost_estimate=pl.CostEstimate(flops=2_000_000, bytes_accessed=2_500_000, transcendentals=2000),
    )(parts, cotangent, gain)


def split_kernel(core_ref, feats_ref, out_ref, sems):
    core = core_ref[0]
    width = feats_ref.shape[1] // (EIGHT * FOUR)
    copies = []
    for p in range(EIGHT):
        for q in range(FOUR):
            block = jnp.where(core == 0, FOUR * p + q, EIGHT * q + p)
            copies.append(
                pltpu.make_async_copy(
                    feats_ref.at[:, pl.ds(pl.multiple_of(block * width, width), width)],
                    out_ref.at[p, :, pl.ds(q * width, width)],
                    sems.at[p, q],
                )
            )
    for copy in copies:
        copy.start()
    for copy in copies:
        copy.wait()


def split_columns(core, feats):
    tokens, width = feats.shape
    return pl.pallas_call(
        split_kernel,
        out_shape=jax.ShapeDtypeStruct((EIGHT, tokens, width // EIGHT), feats.dtype),
        in_specs=[pl.BlockSpec(memory_space=pltpu.SMEM), pl.BlockSpec(memory_space=pltpu.HBM)],
        out_specs=pl.BlockSpec(memory_space=pltpu.HBM),
        scratch_shapes=[pltpu.SemaphoreType.DMA((EIGHT, FOUR))],
        compiler_params=pltpu.CompilerParams(vmem_limit_bytes=60 * 1024 * 1024),
        cost_estimate=pl.CostEstimate(flops=0, bytes_accessed=4 * tokens * width, transcendentals=0),
    )(core, feats)


def gather_rows(x, q):
    out = jnp.zeros((FOUR,) + x.shape, x.dtype)
    for step in range(FOUR):
        piece = x
        if step:
            pairs = [(ring[i], ring[(i + step) % FOUR]) for ring in RINGS_OF_4 for i in range(FOUR)]
            piece = lax.ppermute(x, ALL, pairs)
        out = lax.dynamic_update_index_in_dim(out, piece, lax.rem(q + FOUR - step, FOUR), 0)
    return out


def exchange(x, rings):
    return lax.all_to_all(x, ALL, 0, 0, axis_index_groups=rings)


def gather_by_permutes(x, axis):
    size = lax.axis_size(axis)
    me = lax.axis_index(axis)
    out = jnp.zeros((size,) + x.shape, x.dtype)
    for step in range(size):
        piece = x
        if step:
            piece = lax.ppermute(x, axis, [(i, (i + step) % size) for i in range(size)])
        out = lax.dynamic_update_index_in_dim(out, piece, lax.rem(me + size - step, size), 0)
    return out


def project_kernel(owned_ref, weight_ref, out_ref):
    out_ref[...] = jnp.dot(
        owned_ref[...], weight_ref[...], preferred_element_type=jnp.float32
    ).astype(out_ref.dtype)


def project(owned, weight):
    rows, depth = owned.shape
    columns = weight.shape[1]
    block = rows // 4
    return pl.pallas_call(
        project_kernel,
        grid=(rows // block,),
        out_shape=jax.ShapeDtypeStruct((rows, columns), jnp.bfloat16),
        in_specs=[
            pl.BlockSpec((block, depth), lambda i: (i, 0)),
            pl.BlockSpec((depth, columns), lambda i: (0, 0)),
        ],
        out_specs=pl.BlockSpec((block, columns), lambda i: (i, 0)),
        compiler_params=pltpu.CompilerParams(vmem_limit_bytes=24 * 1024 * 1024),
        cost_estimate=pl.CostEstimate(
            flops=2 * rows * depth * columns,
            bytes_accessed=2 * (rows * depth + depth * columns + rows * columns),
            transcendentals=0,
        ),
    )(owned, weight)


MARKS = 16


def gradient_kernel(owned_ref, slopes_ref, out_ref, exponent_ref):
    @pl.when(pl.program_id(0) == 0)
    def _():
        largest = jnp.max(jnp.abs(slopes_ref[...]).astype(jnp.float32), axis=0, keepdims=True)
        bound = 30.0 * slopes_ref.shape[0] * jnp.max(largest, axis=1, keepdims=True)
        exponent = jnp.ceil(jnp.log2(jnp.maximum(bound, 1e-30))) - 15.0
        exponent_ref[...] = jnp.broadcast_to(exponent, exponent_ref.shape)

    rows = out_ref.shape[1] - MARKS
    sums = lax.dot_general(
        owned_ref[...], slopes_ref[...], (((0,), (0,)), ((), ())), preferred_element_type=jnp.float32
    )
    out_ref[0, :rows] = sums * jnp.exp2(-exponent_ref[0:1, 0:1])
    out_ref[0, rows:] = jnp.broadcast_to(exponent_ref[0:1, 0:1], (MARKS, out_ref.shape[2]))


def gradient_parts(owned, slopes, pieces):
    tokens, width = owned.shape
    columns = slopes.shape[1]
    rows = width // pieces
    return pl.pallas_call(
        gradient_kernel,
        grid=(pieces,),
        out_shape=jax.ShapeDtypeStruct((pieces, rows + MARKS, columns), jnp.float32),
        in_specs=[
            pl.BlockSpec((tokens, rows), lambda i: (0, i)),
            pl.BlockSpec((tokens, columns), lambda i: (0, 0)),
        ],
        out_specs=pl.BlockSpec((1, rows + MARKS, columns), lambda i: (i, 0, 0)),
        scratch_shapes=[pltpu.VMEM((8, 128), jnp.float32)],
        compiler_params=pltpu.CompilerParams(vmem_limit_bytes=24 * 1024 * 1024),
        cost_estimate=pl.CostEstimate(
            flops=2 * tokens * width * columns,
            bytes_accessed=2 * (tokens * width + tokens * columns) + 4 * width * columns,
            transcendentals=0,
        ),
    )(owned, slopes)


def shards(
    activations, key_cotangent, key_gain, local_weight, global_weight, outer_momentum, late_delta
):
    feats = activations[0]
    own_rows = local_weight[0]
    tokens, width = feats.shape
    rows, columns = own_rows.shape
    factor = width ** (-0.5)
    replicas = lax.axis_size(REPLICA)

    core = lax.axis_index("core")
    q = jnp.where(core == 0, lax.axis_index("y_hi"), lax.axis_index("z") // 2)

    owned = exchange(split_columns(core.reshape(1), feats), RINGS_OF_8)
    owned = owned.reshape(EIGHT * tokens, width // EIGHT)
    weight = gather_rows(own_rows.astype(jnp.bfloat16), q).reshape(-1, columns)
    owned, weight = lax.optimization_barrier((owned, weight))
    parts = project(owned, weight).reshape(EIGHT, tokens, columns)

    global_t, momentum_t, late_t = global_weight.T, outer_momentum.T, late_delta.T
    next_momentum_t = keep_rate * momentum_t + late_t
    next_global_t = global_t - outer_rate * (late_t + keep_rate * next_momentum_t)
    parts, new_rows_t = lax.optimization_barrier((parts, next_global_t))
    new_rows_t = gather_by_permutes(gather_by_permutes(new_rows_t, "core"), "y_lo")
    parts = exchange(parts, RINGS_OF_8)
    parts, new_rows_t = lax.optimization_barrier((parts, new_rows_t))
    slopes = key_slopes(parts, key_cotangent[0], key_gain.reshape(1, HEAD), factor)
    slopes, new_rows_t = lax.optimization_barrier((slopes, new_rows_t))
    new_rows_t = gather_by_permutes(new_rows_t, "x")
    new_rows = new_rows_t.transpose(1, 0, 2, 3, 4).reshape(columns, rows).T
    slopes = exchange(slopes, RINGS_OF_8).reshape(EIGHT * tokens, columns)
    slopes, new_rows = lax.optimization_barrier((slopes, new_rows))

    scaled = gradient_parts(owned, slopes, FOUR).astype(jnp.float16)
    pieces = exchange(scaled, RINGS_OF_4)
    unscale = jnp.exp2(pieces[:, rows, 0].astype(jnp.float32)) * factor
    gradient = jnp.sum(pieces[:, :rows].astype(jnp.float32) * unscale[:, None, None], axis=0)

    squares = jnp.sum(gradient * gradient)
    shares = lax.all_to_all(jnp.broadcast_to(squares, (EIGHT * FOUR, 1, 128)), FSDP, 0, 0)
    squares = jnp.sum(shares[:, 0, 0])
    grad_scale = jnp.sqrt(squares / (width * columns) + epsilon)
    after_step = own_rows - inner_rate * gradient / grad_scale

    sent_rows = after_step.T.reshape(replicas, columns // replicas, rows).astype(jnp.float16)
    received = lax.all_to_all(sent_rows, REPLICA, 0, 0).astype(jnp.float32)
    outer_delta_t = global_t - jnp.sum(received, axis=0) / replicas
    next_local = blend_rate * new_rows + (1.0 - blend_rate) * after_step
    return (next_local[None], next_global_t.T, next_momentum_t.T, outer_delta_t.T)


def solution(mesh):
    split = Mesh(mesh.devices.reshape(2, 4, 2, 8, 4), ("y_lo", "x", "core", "z", "y_hi"))
    whole = P(REPLICA, FSDP, None)
    outer = P(FSDP, REPLICA)
    return jax.shard_map(
        shards,
        mesh=split,
        in_specs=(whole, whole, P(), whole, outer, outer, outer),
        out_specs=(whole, outer, outer, outer),
        check_vma=False,
    )
```

```python
import functools

import jax
import jax.numpy as jnp
from jax import lax
from jax.experimental import pallas as pl
from jax.experimental.pallas import tpu as pltpu
from jax.sharding import Mesh
from jax.sharding import PartitionSpec as P

HEAD = 128

inner_rate = 0.5
outer_rate = 0.7
keep_rate = 0.9
blend_rate = 0.5
epsilon = 1e-06

REPLICA = ("y_lo", "x", "core")
FSDP = ("z", "y_hi")
ALL = REPLICA + FSDP

EIGHT, FOUR = 8, 4


def place(core, p, q):
    return (p, q) if core == 0 else (2 * q + p // 4, p % 4)


def device(y_lo, x, core, p, q):
    z, y_hi = place(core, p, q)
    return (((y_lo * 4 + x) * 2 + core) * 8 + z) * 4 + y_hi


TEAMS = [(y_lo, x, core) for y_lo in range(2) for x in range(4) for core in range(2)]
RINGS_OF_8 = [[device(*team, p, q) for p in range(EIGHT)] for team in TEAMS for q in range(FOUR)]
RINGS_OF_4 = [[device(*team, p, q) for q in range(FOUR)] for team in TEAMS for p in range(EIGHT)]


def slope_kernel(factor, parts_ref, cotangent_ref, gain_ref, out_ref):
    pieces = parts_ref.shape[0]
    gain = gain_ref[...]
    for head in range(out_ref.shape[2] // HEAD):
        lanes = slice(head * HEAD, (head + 1) * HEAD)
        hidden = parts_ref[0, :, lanes].astype(jnp.float32)
        for piece in range(1, pieces):
            hidden = hidden + parts_ref[piece, :, lanes].astype(jnp.float32)
        hidden = hidden * factor
        spread = jnp.sqrt(jnp.mean(hidden * hidden, axis=-1, keepdims=True) + epsilon)
        unit = hidden / spread
        slope = cotangent_ref[:, lanes].astype(jnp.float32) * gain
        key_slope = (slope - unit * jnp.mean(slope * unit, axis=-1, keepdims=True)) / spread
        key_slope = key_slope.astype(jnp.bfloat16)
        for piece in range(out_ref.shape[0]):
            out_ref[piece, :, lanes] = key_slope


def key_slopes(parts, cotangent, gain, factor):
    return pl.pallas_call(
        functools.partial(slope_kernel, factor),
        out_shape=jax.ShapeDtypeStruct(parts.shape, jnp.bfloat16),
        compiler_params=pltpu.CompilerParams(vmem_limit_bytes=16 * 1024 * 1024),
        cost_estimate=pl.CostEstimate(flops=2_000_000, bytes_accessed=2_500_000, transcendentals=2000),
    )(parts, cotangent, gain)


def split_kernel(core_ref, feats_ref, out_ref, held, sems, out_sems):
    core = core_ref[0]
    width = feats_ref.shape[1] // (EIGHT * FOUR)
    loads, stores = [], []
    for p in range(EIGHT):
        for q in range(FOUR):
            block = jnp.where(core == 0, FOUR * p + q, EIGHT * q + p)
            loads.append(
                pltpu.make_async_copy(
                    feats_ref.at[:, pl.ds(pl.multiple_of(block * width, width), width)],
                    held.at[p, :, pl.ds(q * width, width)],
                    sems.at[p, q],
                )
            )
        stores.append(pltpu.make_async_copy(held.at[p], out_ref.at[p], out_sems.at[p]))
    for load in loads:
        load.start()
    for p in range(EIGHT):
        for load in loads[FOUR * p : FOUR * (p + 1)]:
            load.wait()
        stores[p].start()
    for store in stores:
        store.wait()


def split_columns(core, feats):
    tokens, width = feats.shape
    shape = (EIGHT, tokens, width // EIGHT)
    return pl.pallas_call(
        split_kernel,
        out_shape=jax.ShapeDtypeStruct(shape, feats.dtype),
        in_specs=[pl.BlockSpec(memory_space=pltpu.SMEM), pl.BlockSpec(memory_space=pltpu.HBM)],
        out_specs=pl.BlockSpec(memory_space=pltpu.HBM),
        scratch_shapes=[
            pltpu.VMEM(shape, feats.dtype),
            pltpu.SemaphoreType.DMA((EIGHT, FOUR)),
            pltpu.SemaphoreType.DMA((EIGHT,)),
        ],
        compiler_params=pltpu.CompilerParams(vmem_limit_bytes=60 * 1024 * 1024),
        cost_estimate=pl.CostEstimate(flops=0, bytes_accessed=4 * tokens * width, transcendentals=0),
    )(core, feats)


def gather_rows(x, q):
    out = jnp.zeros((FOUR,) + x.shape, x.dtype)
    for step in range(FOUR):
        piece = x
        if step:
            pairs = [(ring[i], ring[(i + step) % FOUR]) for ring in RINGS_OF_4 for i in range(FOUR)]
            piece = lax.ppermute(x, ALL, pairs)
        out = lax.dynamic_update_index_in_dim(out, piece, lax.rem(q + FOUR - step, FOUR), 0)
    return out


def exchange(x, rings):
    return lax.all_to_all(x, ALL, 0, 0, axis_index_groups=rings)


def gather_by_permutes(x, axis):
    size = lax.axis_size(axis)
    me = lax.axis_index(axis)
    out = jnp.zeros((size,) + x.shape, x.dtype)
    for step in range(size):
        piece = x
        if step:
            piece = lax.ppermute(x, axis, [(i, (i + step) % size) for i in range(size)])
        out = lax.dynamic_update_index_in_dim(out, piece, lax.rem(me + size - step, size), 0)
    return out


def project_kernel(owned_ref, weight_ref, out_ref):
    out_ref[...] = jnp.dot(
        owned_ref[...], weight_ref[...], preferred_element_type=jnp.float32
    ).astype(out_ref.dtype)


def project(owned, weight):
    rows, depth = owned.shape
    columns = weight.shape[1]
    block = rows // 4
    return pl.pallas_call(
        project_kernel,
        grid=(rows // block,),
        out_shape=jax.ShapeDtypeStruct((rows, columns), jnp.bfloat16),
        in_specs=[
            pl.BlockSpec((block, depth), lambda i: (i, 0)),
            pl.BlockSpec((depth, columns), lambda i: (0, 0)),
        ],
        out_specs=pl.BlockSpec((block, columns), lambda i: (i, 0)),
        compiler_params=pltpu.CompilerParams(vmem_limit_bytes=60 * 1024 * 1024),
        cost_estimate=pl.CostEstimate(
            flops=2 * rows * depth * columns,
            bytes_accessed=2 * (rows * depth + depth * columns + rows * columns),
            transcendentals=0,
        ),
    )(owned, weight)


MARKS = 16


def gradient_kernel(owned_ref, slopes_ref, out_ref, exponent_ref):
    @pl.when(pl.program_id(0) == 0)
    def _():
        largest = jnp.max(jnp.abs(slopes_ref[...]).astype(jnp.float32), axis=0, keepdims=True)
        bound = 30.0 * slopes_ref.shape[0] * jnp.max(largest, axis=1, keepdims=True)
        exponent = jnp.ceil(jnp.log2(jnp.maximum(bound, 1e-30))) - 15.0
        exponent_ref[...] = jnp.broadcast_to(exponent, exponent_ref.shape)

    rows = out_ref.shape[1] - MARKS
    sums = lax.dot_general(
        owned_ref[...], slopes_ref[...], (((0,), (0,)), ((), ())), preferred_element_type=jnp.float32
    )
    out_ref[0, :rows] = sums * jnp.exp2(-exponent_ref[0:1, 0:1])
    out_ref[0, rows:] = jnp.broadcast_to(exponent_ref[0:1, 0:1], (MARKS, out_ref.shape[2]))


def gradient_parts(owned, slopes, pieces):
    tokens, width = owned.shape
    columns = slopes.shape[1]
    rows = width // pieces
    return pl.pallas_call(
        gradient_kernel,
        grid=(pieces,),
        out_shape=jax.ShapeDtypeStruct((pieces, rows + MARKS, columns), jnp.float32),
        in_specs=[
            pl.BlockSpec((tokens, rows), lambda i: (0, i)),
            pl.BlockSpec((tokens, columns), lambda i: (0, 0)),
        ],
        out_specs=pl.BlockSpec((1, rows + MARKS, columns), lambda i: (i, 0, 0)),
        scratch_shapes=[pltpu.VMEM((8, 128), jnp.float32)],
        compiler_params=pltpu.CompilerParams(vmem_limit_bytes=24 * 1024 * 1024),
        cost_estimate=pl.CostEstimate(
            flops=2 * tokens * width * columns,
            bytes_accessed=2 * (tokens * width + tokens * columns) + 4 * width * columns,
            transcendentals=0,
        ),
    )(owned, slopes)


def shards(
    activations, key_cotangent, key_gain, local_weight, global_weight, outer_momentum, late_delta
):
    feats = activations[0]
    own_rows = local_weight[0]
    tokens, width = feats.shape
    rows, columns = own_rows.shape
    factor = width ** (-0.5)
    replicas = lax.axis_size(REPLICA)

    core = lax.axis_index("core")
    q = jnp.where(core == 0, lax.axis_index("y_hi"), lax.axis_index("z") // 2)

    owned = exchange(split_columns(core.reshape(1), feats), RINGS_OF_8)
    owned = owned.reshape(EIGHT * tokens, width // EIGHT)
    weight = gather_rows(own_rows.astype(jnp.bfloat16), q).reshape(-1, columns)
    owned, weight = lax.optimization_barrier((owned, weight))
    parts = project(owned, weight).reshape(EIGHT, tokens, columns)

    global_t, momentum_t, late_t = global_weight.T, outer_momentum.T, late_delta.T
    next_momentum_t = keep_rate * momentum_t + late_t
    next_global_t = global_t - outer_rate * (late_t + keep_rate * next_momentum_t)
    parts, new_rows_t = lax.optimization_barrier((parts, next_global_t))
    new_rows_t = gather_by_permutes(gather_by_permutes(new_rows_t, "core"), "y_lo")
    parts = exchange(parts, RINGS_OF_8)
    parts, new_rows_t = lax.optimization_barrier((parts, new_rows_t))
    slopes = key_slopes(parts, key_cotangent[0], key_gain.reshape(1, HEAD), factor)
    slopes, new_rows_t = lax.optimization_barrier((slopes, new_rows_t))
    new_rows_t = gather_by_permutes(new_rows_t, "x")
    new_rows = new_rows_t.transpose(1, 0, 2, 3, 4).reshape(columns, rows).T
    slopes = exchange(slopes, RINGS_OF_8).reshape(EIGHT * tokens, columns)
    slopes, new_rows = lax.optimization_barrier((slopes, new_rows))

    scaled = gradient_parts(owned, slopes, FOUR).astype(jnp.float16)
    pieces = exchange(scaled, RINGS_OF_4)
    unscale = jnp.exp2(pieces[:, rows, 0].astype(jnp.float32)) * factor
    gradient = jnp.sum(pieces[:, :rows].astype(jnp.float32) * unscale[:, None, None], axis=0)

    squares = jnp.sum(gradient * gradient)
    shares = lax.all_to_all(jnp.broadcast_to(squares, (EIGHT * FOUR, 1, 128)), FSDP, 0, 0)
    squares = jnp.sum(shares[:, 0, 0])
    grad_scale = jnp.sqrt(squares / (width * columns) + epsilon)
    after_step = own_rows - inner_rate * gradient / grad_scale

    sent_rows = after_step.T.reshape(replicas, columns // replicas, rows).astype(jnp.float16)
    received = lax.all_to_all(sent_rows, REPLICA, 0, 0).astype(jnp.float32)
    outer_delta_t = global_t - jnp.sum(received, axis=0) / replicas
    next_local = blend_rate * new_rows + (1.0 - blend_rate) * after_step
    return (next_local[None], next_global_t.T, next_momentum_t.T, outer_delta_t.T)


def solution(mesh):
    split = Mesh(mesh.devices.reshape(2, 4, 2, 8, 4), ("y_lo", "x", "core", "z", "y_hi"))
    whole = P(REPLICA, FSDP, None)
    outer = P(FSDP, REPLICA)
    return jax.shard_map(
        shards,
        mesh=split,
        in_specs=(whole, whole, P(), whole, outer, outer, outer),
        out_specs=(whole, outer, outer, outer),
        check_vma=False,
    )
```

```python
import functools

import jax
import jax.numpy as jnp
from jax import lax
from jax.experimental import pallas as pl
from jax.experimental.pallas import tpu as pltpu
from jax.sharding import Mesh
from jax.sharding import PartitionSpec as P

HEAD = 128

inner_rate = 0.5
outer_rate = 0.7
keep_rate = 0.9
blend_rate = 0.5
epsilon = 1e-06

REPLICA = ("y_lo", "x", "core")
FSDP = ("z", "y_hi")
ALL = REPLICA + FSDP

EIGHT, FOUR = 8, 4


def place(core, p, q):
    return (p, q) if core == 0 else (2 * q + p // 4, p % 4)


def device(y_lo, x, core, p, q):
    z, y_hi = place(core, p, q)
    return (((y_lo * 4 + x) * 2 + core) * 8 + z) * 4 + y_hi


TEAMS = [(y_lo, x, core) for y_lo in range(2) for x in range(4) for core in range(2)]
RINGS_OF_8 = [[device(*team, p, q) for p in range(EIGHT)] for team in TEAMS for q in range(FOUR)]
RINGS_OF_4 = [[device(*team, p, q) for q in range(FOUR)] for team in TEAMS for p in range(EIGHT)]


def slope_kernel(factor, parts_ref, cotangent_ref, gain_ref, out_ref):
    pieces = parts_ref.shape[0]
    gain = gain_ref[...]
    for head in range(out_ref.shape[1] // HEAD):
        lanes = slice(head * HEAD, (head + 1) * HEAD)
        hidden = parts_ref[0, :, lanes].astype(jnp.float32)
        for piece in range(1, pieces):
            hidden = hidden + parts_ref[piece, :, lanes].astype(jnp.float32)
        hidden = hidden * factor
        spread = jnp.sqrt(jnp.mean(hidden * hidden, axis=-1, keepdims=True) + epsilon)
        unit = hidden / spread
        slope = cotangent_ref[:, lanes].astype(jnp.float32) * gain
        key_slope = (slope - unit * jnp.mean(slope * unit, axis=-1, keepdims=True)) / spread
        key_slope = key_slope.T.astype(jnp.bfloat16)
        for piece in range(out_ref.shape[0]):
            out_ref[piece, lanes, :] = key_slope


def key_slopes(parts, cotangent, gain, factor):
    return pl.pallas_call(
        functools.partial(slope_kernel, factor),
        out_shape=jax.ShapeDtypeStruct((parts.shape[0],) + parts.shape[:0:-1], jnp.bfloat16),
        compiler_params=pltpu.CompilerParams(vmem_limit_bytes=8 * 1024 * 1024),
        cost_estimate=pl.CostEstimate(flops=2_000_000, bytes_accessed=2_500_000, transcendentals=2000),
    )(parts, cotangent, gain)


def split_kernel(core_ref, feats_ref, out_ref, held, sems, out_sems):
    core = core_ref[0]
    width = feats_ref.shape[1] // (EIGHT * FOUR)
    loads, stores = [], []
    for p in range(EIGHT):
        for q in range(FOUR):
            block = jnp.where(core == 0, FOUR * p + q, EIGHT * q + p)
            loads.append(
                pltpu.make_async_copy(
                    feats_ref.at[:, pl.ds(pl.multiple_of(block * width, width), width)],
                    held.at[p, :, pl.ds(q * width, width)],
                    sems.at[p, q],
                )
            )
        stores.append(pltpu.make_async_copy(held.at[p], out_ref.at[p], out_sems.at[p]))
    for load in loads:
        load.start()
    for p in range(EIGHT):
        for load in loads[FOUR * p : FOUR * (p + 1)]:
            load.wait()
        stores[p].start()
    for store in stores:
        store.wait()


def split_columns(core, feats):
    tokens, width = feats.shape
    shape = (EIGHT, tokens, width // EIGHT)
    return pl.pallas_call(
        split_kernel,
        out_shape=jax.ShapeDtypeStruct(shape, feats.dtype),
        in_specs=[pl.BlockSpec(memory_space=pltpu.SMEM), pl.BlockSpec(memory_space=pltpu.HBM)],
        out_specs=pl.BlockSpec(memory_space=pltpu.HBM),
        scratch_shapes=[
            pltpu.VMEM(shape, feats.dtype),
            pltpu.SemaphoreType.DMA((EIGHT, FOUR)),
            pltpu.SemaphoreType.DMA((EIGHT,)),
        ],
        compiler_params=pltpu.CompilerParams(vmem_limit_bytes=60 * 1024 * 1024),
        cost_estimate=pl.CostEstimate(flops=0, bytes_accessed=4 * tokens * width, transcendentals=0),
    )(core, feats)


def gather_rows(x):
    out = [x]
    for step in range(1, FOUR):
        pairs = [(ring[i], ring[(i + step) % FOUR]) for ring in RINGS_OF_4 for i in range(FOUR)]
        out.append(lax.ppermute(x, ALL, pairs))
    return out


def exchange(x, rings):
    return lax.all_to_all(x, ALL, 0, 0, axis_index_groups=rings)


def gather_by_permutes(x, axis):
    size = lax.axis_size(axis)
    me = lax.axis_index(axis)
    out = jnp.zeros((size,) + x.shape, x.dtype)
    for step in range(size):
        piece = x
        if step:
            piece = lax.ppermute(x, axis, [(i, (i + step) % size) for i in range(size)])
        out = lax.dynamic_update_index_in_dim(out, piece, lax.rem(me + size - step, size), 0)
    return out


def project_kernel(q_ref, owned_ref, *refs):
    pieces, out_ref, weight_ref = refs[:-2], refs[-2], refs[-1]
    width = pieces[0].shape[0]
    for step, piece in enumerate(pieces):
        first = lax.rem(q_ref[0] + len(pieces) - step, len(pieces)) * width
        weight_ref[pl.ds(pl.multiple_of(first, width), width), :] = piece[...]
    block = owned_ref.shape[0] // 4
    for i in range(4):
        rows = slice(i * block, (i + 1) * block)
        out_ref[rows, :] = jnp.dot(
            owned_ref[rows, :], weight_ref[...], preferred_element_type=jnp.float32
        ).astype(out_ref.dtype)


def project(q, owned, pieces):
    rows, depth = owned.shape
    columns = pieces[0].shape[1]
    return pl.pallas_call(
        project_kernel,
        out_shape=jax.ShapeDtypeStruct((rows, columns), jnp.bfloat16),
        in_specs=[pl.BlockSpec(memory_space=pltpu.SMEM)]
        + [pl.BlockSpec(memory_space=pltpu.VMEM)] * (1 + len(pieces)),
        out_specs=pl.BlockSpec(memory_space=pltpu.VMEM),
        scratch_shapes=[pltpu.VMEM((depth, columns), jnp.bfloat16)],
        compiler_params=pltpu.CompilerParams(vmem_limit_bytes=12 * 1024 * 1024),
        cost_estimate=pl.CostEstimate(
            flops=2 * rows * depth * columns,
            bytes_accessed=2 * (rows * depth + depth * columns + rows * columns),
            transcendentals=0,
        ),
    )(q, owned, *pieces)


MARKS = 16


def gradient_kernel(owned_ref, slopes_ref, out_ref, all_slopes_ref):
    pieces, columns, tokens = slopes_ref.shape
    largest = jnp.abs(slopes_ref[0])
    for piece in range(pieces):
        all_slopes_ref[:, piece * tokens : (piece + 1) * tokens] = slopes_ref[piece]
        if piece:
            largest = jnp.maximum(largest, jnp.abs(slopes_ref[piece]))
    largest = jnp.max(largest.astype(jnp.float32), axis=0, keepdims=True)
    bound = 30.0 * owned_ref.shape[0] * jnp.max(largest, axis=1, keepdims=True)
    exponent = jnp.ceil(jnp.log2(jnp.maximum(bound, 1e-30))) - 15.0
    receivers, _, rows = out_ref.shape
    for i in range(receivers):
        sums = jnp.dot(
            all_slopes_ref[...],
            owned_ref[:, i * rows : (i + 1) * rows],
            preferred_element_type=jnp.float32,
        )
        out_ref[i, :columns] = sums * jnp.exp2(-exponent)
        out_ref[i, columns:] = jnp.broadcast_to(exponent, (MARKS, rows))


def gradient_parts(owned, slopes, receivers):
    tokens, width = owned.shape
    columns = slopes.shape[1]
    rows = width // receivers
    return pl.pallas_call(
        gradient_kernel,
        out_shape=jax.ShapeDtypeStruct((receivers, columns + MARKS, rows), jnp.float32),
        in_specs=[pl.BlockSpec(memory_space=pltpu.VMEM)] * 2,
        out_specs=pl.BlockSpec(memory_space=pltpu.VMEM),
        scratch_shapes=[pltpu.VMEM((columns, tokens), jnp.bfloat16)],
        compiler_params=pltpu.CompilerParams(vmem_limit_bytes=12 * 1024 * 1024),
        cost_estimate=pl.CostEstimate(
            flops=2 * tokens * width * columns,
            bytes_accessed=2 * (tokens * width + tokens * columns) + 4 * width * columns,
            transcendentals=0,
        ),
    )(owned, slopes)


def squares_kernel(gradient_ref, out_ref):
    gradient = gradient_ref[...]
    columns = jnp.sum(gradient * gradient, axis=0, keepdims=True)
    out_ref[...] = jnp.broadcast_to(jnp.sum(columns, axis=1, keepdims=True), out_ref.shape)


def squares_for_all(gradient, receivers):
    return pl.pallas_call(
        squares_kernel,
        out_shape=jax.ShapeDtypeStruct((receivers, 8, 128), jnp.float32),
        compiler_params=pltpu.CompilerParams(vmem_limit_bytes=8 * 1024 * 1024),
        cost_estimate=pl.CostEstimate(flops=2 * gradient.size, bytes_accessed=4 * gradient.size, transcendentals=0),
    )(gradient)


def step_kernel(size, shares_ref, own_ref, gradient_ref, after_ref):
    rate = inner_rate / jnp.sqrt(jnp.sum(shares_ref[...], axis=0) / size + epsilon)
    after_ref[...] = own_ref[...].T - rate[0:1, 0:1] * gradient_ref[...]


def step(shares, own_rows, gradient_t):
    size = shares.shape[0] * own_rows.size
    return pl.pallas_call(
        functools.partial(step_kernel, size),
        out_shape=jax.ShapeDtypeStruct(gradient_t.shape, jnp.float32),
        compiler_params=pltpu.CompilerParams(vmem_limit_bytes=8 * 1024 * 1024),
        cost_estimate=pl.CostEstimate(flops=2 * own_rows.size, bytes_accessed=12 * own_rows.size, transcendentals=0),
    )(shares, own_rows, gradient_t)


def blend_kernel(after_ref, new_ref, out_ref):
    xs, y_los, cores, width, rows = new_ref.shape
    for y_lo in range(y_los):
        for x in range(xs):
            first = (y_lo * xs + x) * cores * width
            part = slice(first, first + cores * width)
            new = new_ref[x, y_lo].reshape(cores * width, rows)
            out_ref[:, part] = (blend_rate * new + (1.0 - blend_rate) * after_ref[part, :]).T


def blend(after_step_t, new_rows_t):
    return pl.pallas_call(
        blend_kernel,
        out_shape=jax.ShapeDtypeStruct(after_step_t.shape[::-1], jnp.float32),
        compiler_params=pltpu.CompilerParams(vmem_limit_bytes=8 * 1024 * 1024),
        cost_estimate=pl.CostEstimate(
            flops=3 * after_step_t.size, bytes_accessed=12 * after_step_t.size, transcendentals=0
        ),
    )(after_step_t, new_rows_t)


def shards(
    activations, key_cotangent, key_gain, local_weight, global_weight, outer_momentum, late_delta
):
    feats = activations[0]
    own_rows = local_weight[0]
    tokens, width = feats.shape
    rows, columns = own_rows.shape
    factor = width ** (-0.5)
    replicas = lax.axis_size(REPLICA)

    core = lax.axis_index("core")
    q = jnp.where(core == 0, lax.axis_index("y_hi"), lax.axis_index("z") // 2)

    owned = exchange(split_columns(core.reshape(1), feats), RINGS_OF_8)
    owned = owned.reshape(EIGHT * tokens, width // EIGHT)
    weight = gather_rows(own_rows.astype(jnp.bfloat16))

    global_t, momentum_t, late_t = global_weight.T, outer_momentum.T, late_delta.T
    next_momentum_t = keep_rate * momentum_t + late_t
    next_global_t = global_t - outer_rate * (late_t + keep_rate * next_momentum_t)
    new_rows_t = gather_by_permutes(gather_by_permutes(next_global_t, "core"), "y_lo")
    owned, weight, new_rows_t = lax.optimization_barrier((owned, weight, new_rows_t))
    parts = project(q.reshape(1), owned, weight).reshape(EIGHT, tokens, columns)
    parts = exchange(parts, RINGS_OF_8)
    slopes = key_slopes(parts, key_cotangent[0], key_gain.reshape(1, HEAD), factor)
    slopes = exchange(slopes, RINGS_OF_8)

    scaled = gradient_parts(owned, slopes, FOUR).astype(jnp.float16)
    scaled, new_rows_t = lax.optimization_barrier((scaled, new_rows_t))
    new_rows_t = gather_by_permutes(new_rows_t, "x")
    pieces = exchange(scaled, RINGS_OF_4)
    pieces, new_rows_t = lax.optimization_barrier((pieces, new_rows_t))
    unscale = jnp.exp2(pieces[:, columns, 0].astype(jnp.float32)) * factor
    gradient_t = jnp.sum(pieces[:, :columns].astype(jnp.float32) * unscale[:, None, None], axis=0)
    shares = lax.all_to_all(squares_for_all(gradient_t, EIGHT * FOUR), FSDP, 0, 0)
    after_step_t = step(shares, own_rows, gradient_t)

    sent_rows = after_step_t.reshape(replicas, columns // replicas, rows)
    received = lax.all_to_all(sent_rows.astype(jnp.float16), REPLICA, 0, 0).astype(jnp.float32)
    outer_delta_t = global_t - jnp.sum(received, axis=0) / replicas
    next_local = blend(after_step_t, new_rows_t)
    return (next_local[None], next_global_t.T, next_momentum_t.T, outer_delta_t.T)


def solution(mesh):
    split = Mesh(mesh.devices.reshape(2, 4, 2, 8, 4), ("y_lo", "x", "core", "z", "y_hi"))
    whole = P(REPLICA, FSDP, None)
    outer = P(FSDP, REPLICA)
    return jax.shard_map(
        shards,
        mesh=split,
        in_specs=(whole, whole, P(), whole, outer, outer, outer),
        out_specs=(whole, outer, outer, outer),
        check_vma=False,
    )
```

```python
import functools

import jax
import jax.numpy as jnp
from jax import lax
from jax.experimental import pallas as pl
from jax.experimental.pallas import tpu as pltpu
from jax.sharding import Mesh
from jax.sharding import PartitionSpec as P

HEAD = 128

inner_rate = 0.5
outer_rate = 0.7
keep_rate = 0.9
blend_rate = 0.5
epsilon = 1e-06

REPLICA = ("y_lo", "x", "core")
FSDP = ("z", "y_hi")
ALL = REPLICA + FSDP

EIGHT, FOUR = 8, 4


def place(core, p, q):
    return (p, q) if core == 0 else (2 * q + p // 4, p % 4)


def device(y_lo, x, core, p, q):
    z, y_hi = place(core, p, q)
    return (((y_lo * 4 + x) * 2 + core) * 8 + z) * 4 + y_hi


TEAMS = [(y_lo, x, core) for y_lo in range(2) for x in range(4) for core in range(2)]
RINGS_OF_8 = [[device(*team, p, q) for p in range(EIGHT)] for team in TEAMS for q in range(FOUR)]
RINGS_OF_4 = [[device(*team, p, q) for q in range(FOUR)] for team in TEAMS for p in range(EIGHT)]


def slope_kernel(factor, parts_ref, cotangent_ref, gain_ref, out_ref):
    pieces = parts_ref.shape[0]
    gain = gain_ref[...]
    for head in range(out_ref.shape[1] // HEAD):
        lanes = slice(head * HEAD, (head + 1) * HEAD)
        hidden = parts_ref[0, :, lanes].astype(jnp.float32)
        for piece in range(1, pieces):
            hidden = hidden + parts_ref[piece, :, lanes].astype(jnp.float32)
        hidden = hidden * factor
        spread = jnp.sqrt(jnp.mean(hidden * hidden, axis=-1, keepdims=True) + epsilon)
        unit = hidden / spread
        slope = cotangent_ref[:, lanes].astype(jnp.float32) * gain
        key_slope = (slope - unit * jnp.mean(slope * unit, axis=-1, keepdims=True)) / spread
        key_slope = key_slope.T.astype(jnp.bfloat16)
        for piece in range(out_ref.shape[0]):
            out_ref[piece, lanes, :] = key_slope


def key_slopes(parts, cotangent, gain, factor):
    return pl.pallas_call(
        functools.partial(slope_kernel, factor),
        out_shape=jax.ShapeDtypeStruct((parts.shape[0],) + parts.shape[:0:-1], jnp.bfloat16),
        compiler_params=pltpu.CompilerParams(vmem_limit_bytes=8 * 1024 * 1024),
        cost_estimate=pl.CostEstimate(flops=2_000_000, bytes_accessed=2_500_000, transcendentals=2000),
    )(parts, cotangent, gain)


def split_kernel(core_ref, feats_ref, out_ref, held, sems, out_sems):
    core = core_ref[0]
    width = feats_ref.shape[1] // (EIGHT * FOUR)
    loads, stores = [], []
    for p in range(EIGHT):
        for q in range(FOUR):
            block = jnp.where(core == 0, FOUR * p + q, EIGHT * q + p)
            loads.append(
                pltpu.make_async_copy(
                    feats_ref.at[:, pl.ds(pl.multiple_of(block * width, width), width)],
                    held.at[p, :, pl.ds(q * width, width)],
                    sems.at[p, q],
                )
            )
        stores.append(pltpu.make_async_copy(held.at[p], out_ref.at[p], out_sems.at[p]))
    for load in loads:
        load.start()
    for p in range(EIGHT):
        for load in loads[FOUR * p : FOUR * (p + 1)]:
            load.wait()
        stores[p].start()
    for store in stores:
        store.wait()


def split_columns(core, feats):
    tokens, width = feats.shape
    shape = (EIGHT, tokens, width // EIGHT)
    return pl.pallas_call(
        split_kernel,
        out_shape=jax.ShapeDtypeStruct(shape, feats.dtype),
        in_specs=[pl.BlockSpec(memory_space=pltpu.SMEM), pl.BlockSpec(memory_space=pltpu.HBM)],
        out_specs=pl.BlockSpec(memory_space=pltpu.HBM),
        scratch_shapes=[
            pltpu.VMEM(shape, feats.dtype),
            pltpu.SemaphoreType.DMA((EIGHT, FOUR)),
            pltpu.SemaphoreType.DMA((EIGHT,)),
        ],
        compiler_params=pltpu.CompilerParams(vmem_limit_bytes=60 * 1024 * 1024),
        cost_estimate=pl.CostEstimate(flops=0, bytes_accessed=4 * tokens * width, transcendentals=0),
    )(core, feats)


def gather_rows(x):
    out = [x]
    for step in range(1, FOUR):
        pairs = [(ring[i], ring[(i + step) % FOUR]) for ring in RINGS_OF_4 for i in range(FOUR)]
        out.append(lax.ppermute(x, ALL, pairs))
    return out


def exchange(x, rings):
    return lax.all_to_all(x, ALL, 0, 0, axis_index_groups=rings)


def gather_by_permutes(x, axis):
    size = lax.axis_size(axis)
    me = lax.axis_index(axis)
    out = jnp.zeros((size,) + x.shape, x.dtype)
    for step in range(size):
        piece = x
        if step:
            piece = lax.ppermute(x, axis, [(i, (i + step) % size) for i in range(size)])
        out = lax.dynamic_update_index_in_dim(out, piece, lax.rem(me + size - step, size), 0)
    return out


def project_kernel(q_ref, owned_ref, *refs):
    pieces, out_ref, weight_ref = refs[:-2], refs[-2], refs[-1]
    width = pieces[0].shape[0]
    for step, piece in enumerate(pieces):
        first = lax.rem(q_ref[0] + len(pieces) - step, len(pieces)) * width
        weight_ref[pl.ds(pl.multiple_of(first, width), width), :] = piece[...]
    block = owned_ref.shape[0] // 4
    for i in range(4):
        rows = slice(i * block, (i + 1) * block)
        out_ref[rows, :] = jnp.dot(
            owned_ref[rows, :], weight_ref[...], preferred_element_type=jnp.float32
        ).astype(out_ref.dtype)


def project(q, owned, pieces):
    rows, depth = owned.shape
    columns = pieces[0].shape[1]
    return pl.pallas_call(
        project_kernel,
        out_shape=jax.ShapeDtypeStruct((rows, columns), jnp.bfloat16),
        in_specs=[pl.BlockSpec(memory_space=pltpu.SMEM)]
        + [pl.BlockSpec(memory_space=pltpu.VMEM)] * (1 + len(pieces)),
        out_specs=pl.BlockSpec(memory_space=pltpu.VMEM),
        scratch_shapes=[pltpu.VMEM((depth, columns), jnp.bfloat16)],
        compiler_params=pltpu.CompilerParams(vmem_limit_bytes=12 * 1024 * 1024),
        cost_estimate=pl.CostEstimate(
            flops=2 * rows * depth * columns,
            bytes_accessed=2 * (rows * depth + depth * columns + rows * columns),
            transcendentals=0,
        ),
    )(q, owned, *pieces)


MARKS = 16


def gradient_kernel(owned_ref, slopes_ref, out_ref, all_slopes_ref):
    pieces, columns, tokens = slopes_ref.shape
    largest = jnp.abs(slopes_ref[0])
    for piece in range(pieces):
        all_slopes_ref[:, piece * tokens : (piece + 1) * tokens] = slopes_ref[piece]
        if piece:
            largest = jnp.maximum(largest, jnp.abs(slopes_ref[piece]))
    largest = jnp.max(largest.astype(jnp.float32), axis=0, keepdims=True)
    bound = 30.0 * owned_ref.shape[0] * jnp.max(largest, axis=1, keepdims=True)
    exponent = jnp.ceil(jnp.log2(jnp.maximum(bound, 1e-30))) - 15.0
    receivers, _, rows = out_ref.shape
    for i in range(receivers):
        sums = jnp.dot(
            all_slopes_ref[...],
            owned_ref[:, i * rows : (i + 1) * rows],
            preferred_element_type=jnp.float32,
        )
        out_ref[i, :columns] = sums * jnp.exp2(-exponent)
        out_ref[i, columns:] = jnp.broadcast_to(exponent, (MARKS, rows))


def gradient_parts(owned, slopes, receivers):
    tokens, width = owned.shape
    columns = slopes.shape[1]
    rows = width // receivers
    return pl.pallas_call(
        gradient_kernel,
        out_shape=jax.ShapeDtypeStruct((receivers, columns + MARKS, rows), jnp.float32),
        in_specs=[pl.BlockSpec(memory_space=pltpu.VMEM)] * 2,
        out_specs=pl.BlockSpec(memory_space=pltpu.VMEM),
        scratch_shapes=[pltpu.VMEM((columns, tokens), jnp.bfloat16)],
        compiler_params=pltpu.CompilerParams(vmem_limit_bytes=12 * 1024 * 1024),
        cost_estimate=pl.CostEstimate(
            flops=2 * tokens * width * columns,
            bytes_accessed=2 * (tokens * width + tokens * columns) + 4 * width * columns,
            transcendentals=0,
        ),
    )(owned, slopes)


def squares_kernel(gradient_ref, out_ref):
    gradient = gradient_ref[...]
    columns = jnp.sum(gradient * gradient, axis=0, keepdims=True)
    out_ref[...] = jnp.broadcast_to(jnp.sum(columns, axis=1, keepdims=True), out_ref.shape)


def squares_for_all(gradient, receivers):
    return pl.pallas_call(
        squares_kernel,
        out_shape=jax.ShapeDtypeStruct((receivers, 8, 128), jnp.float32),
        compiler_params=pltpu.CompilerParams(vmem_limit_bytes=8 * 1024 * 1024),
        cost_estimate=pl.CostEstimate(flops=2 * gradient.size, bytes_accessed=4 * gradient.size, transcendentals=0),
    )(gradient)


def step_kernel(size, shares_ref, own_ref, gradient_ref, after_ref):
    rate = inner_rate / jnp.sqrt(jnp.sum(shares_ref[...], axis=0) / size + epsilon)
    after_ref[...] = own_ref[...].T - rate[0:1, 0:1] * gradient_ref[...]


def step(shares, own_rows, gradient_t):
    size = shares.shape[0] * own_rows.size
    return pl.pallas_call(
        functools.partial(step_kernel, size),
        out_shape=jax.ShapeDtypeStruct(gradient_t.shape, jnp.float32),
        compiler_params=pltpu.CompilerParams(vmem_limit_bytes=8 * 1024 * 1024),
        cost_estimate=pl.CostEstimate(flops=2 * own_rows.size, bytes_accessed=12 * own_rows.size, transcendentals=0),
    )(shares, own_rows, gradient_t)


def blend_kernel(after_ref, new_ref, out_ref):
    xs, y_los, cores, width, rows = new_ref.shape
    for y_lo in range(y_los):
        for x in range(xs):
            first = (y_lo * xs + x) * cores * width
            part = slice(first, first + cores * width)
            new = new_ref[x, y_lo].reshape(cores * width, rows)
            out_ref[:, part] = (blend_rate * new + (1.0 - blend_rate) * after_ref[part, :]).T


def blend(after_step_t, new_rows_t):
    return pl.pallas_call(
        blend_kernel,
        out_shape=jax.ShapeDtypeStruct(after_step_t.shape[::-1], jnp.float32),
        compiler_params=pltpu.CompilerParams(vmem_limit_bytes=8 * 1024 * 1024),
        cost_estimate=pl.CostEstimate(
            flops=3 * after_step_t.size, bytes_accessed=12 * after_step_t.size, transcendentals=0
        ),
    )(after_step_t, new_rows_t)


def shards(
    activations, key_cotangent, key_gain, local_weight, global_weight, outer_momentum, late_delta
):
    feats = activations[0]
    own_rows = local_weight[0]
    tokens, width = feats.shape
    rows, columns = own_rows.shape
    factor = width ** (-0.5)
    replicas = lax.axis_size(REPLICA)

    core = lax.axis_index("core")
    q = jnp.where(core == 0, lax.axis_index("y_hi"), lax.axis_index("z") // 2)

    owned = exchange(split_columns(core.reshape(1), feats), RINGS_OF_8)
    owned = owned.reshape(EIGHT * tokens, width // EIGHT)
    weight = gather_rows(own_rows.astype(jnp.bfloat16))

    global_t, momentum_t, late_t = global_weight.T, outer_momentum.T, late_delta.T
    next_momentum_t = keep_rate * momentum_t + late_t
    next_global_t = global_t - outer_rate * (late_t + keep_rate * next_momentum_t)
    new_rows_t = gather_by_permutes(gather_by_permutes(next_global_t, "core"), "y_lo")
    owned, weight, new_rows_t = lax.optimization_barrier((owned, weight, new_rows_t))
    parts = project(q.reshape(1), owned, weight).reshape(EIGHT, tokens, columns)
    parts = exchange(parts, RINGS_OF_8)
    slopes = key_slopes(parts, key_cotangent[0], key_gain.reshape(1, HEAD), factor)
    slopes, new_rows_t = lax.optimization_barrier((slopes, new_rows_t))
    new_rows_t = gather_by_permutes(new_rows_t, "x")
    slopes = exchange(slopes, RINGS_OF_8)
    slopes, new_rows_t = lax.optimization_barrier((slopes, new_rows_t))

    scaled = gradient_parts(owned, slopes, FOUR).astype(jnp.float16)
    pieces = exchange(scaled, RINGS_OF_4)
    unscale = jnp.exp2(pieces[:, columns, 0].astype(jnp.float32)) * factor
    gradient_t = jnp.sum(pieces[:, :columns].astype(jnp.float32) * unscale[:, None, None], axis=0)
    shares = lax.all_to_all(squares_for_all(gradient_t, EIGHT * FOUR), FSDP, 0, 0)
    after_step_t = step(shares, own_rows, gradient_t)

    sent_rows = after_step_t.reshape(replicas, columns // replicas, rows)
    received = lax.all_to_all(sent_rows.astype(jnp.float16), REPLICA, 0, 0).astype(jnp.float32)
    outer_delta_t = global_t - jnp.sum(received, axis=0) / replicas
    next_local = blend(after_step_t, new_rows_t)
    return (next_local[None], next_global_t.T, next_momentum_t.T, outer_delta_t.T)


def solution(mesh):
    split = Mesh(mesh.devices.reshape(2, 4, 2, 8, 4), ("y_lo", "x", "core", "z", "y_hi"))
    whole = P(REPLICA, FSDP, None)
    outer = P(FSDP, REPLICA)
    return jax.shard_map(
        shards,
        mesh=split,
        in_specs=(whole, whole, P(), whole, outer, outer, outer),
        out_specs=(whole, outer, outer, outer),
        check_vma=False,
    )
```

```python
import functools

import jax
import jax.numpy as jnp
from jax import lax
from jax.experimental import pallas as pl
from jax.experimental.pallas import tpu as pltpu
from jax.sharding import Mesh
from jax.sharding import PartitionSpec as P

HEAD = 128

inner_rate = 0.5
outer_rate = 0.7
keep_rate = 0.9
blend_rate = 0.5
epsilon = 1e-06

REPLICA = ("y_lo", "x", "core")
FSDP = ("z", "y_hi")
ALL = REPLICA + FSDP

EIGHT, FOUR = 8, 4


def place(core, p, q):
    return (p, q) if core == 0 else (2 * q + p // 4, p % 4)


def device(y_lo, x, core, p, q):
    z, y_hi = place(core, p, q)
    return (((y_lo * 4 + x) * 2 + core) * 8 + z) * 4 + y_hi


TEAMS = [(y_lo, x, core) for y_lo in range(2) for x in range(4) for core in range(2)]
RINGS_OF_8 = [[device(*team, p, q) for p in range(EIGHT)] for team in TEAMS for q in range(FOUR)]
RINGS_OF_4 = [[device(*team, p, q) for q in range(FOUR)] for team in TEAMS for p in range(EIGHT)]


def slope_kernel(factor, parts_ref, cotangent_ref, gain_ref, out_ref):
    pieces = parts_ref.shape[0]
    gain = gain_ref[...]
    for head in range(out_ref.shape[1] // HEAD):
        lanes = slice(head * HEAD, (head + 1) * HEAD)
        hidden = parts_ref[0, :, lanes].astype(jnp.float32)
        for piece in range(1, pieces):
            hidden = hidden + parts_ref[piece, :, lanes].astype(jnp.float32)
        hidden = hidden * factor
        spread = jnp.sqrt(jnp.mean(hidden * hidden, axis=-1, keepdims=True) + epsilon)
        unit = hidden / spread
        slope = cotangent_ref[:, lanes].astype(jnp.float32) * gain
        key_slope = (slope - unit * jnp.mean(slope * unit, axis=-1, keepdims=True)) / spread
        key_slope = key_slope.T.astype(jnp.bfloat16)
        for piece in range(out_ref.shape[0]):
            out_ref[piece, lanes, :] = key_slope


def key_slopes(parts, cotangent, gain, factor):
    return pl.pallas_call(
        functools.partial(slope_kernel, factor),
        out_shape=jax.ShapeDtypeStruct((parts.shape[0],) + parts.shape[:0:-1], jnp.bfloat16),
        compiler_params=pltpu.CompilerParams(vmem_limit_bytes=8 * 1024 * 1024),
        cost_estimate=pl.CostEstimate(flops=2_000_000, bytes_accessed=2_500_000, transcendentals=2000),
    )(parts, cotangent, gain)


def split_kernel(core_ref, feats_ref, out_ref, held, sems, out_sems):
    width = feats_ref.shape[1] // (EIGHT * FOUR)

    def load(first, size, p, q):
        return pltpu.make_async_copy(
            feats_ref.at[:, pl.ds(first * width, size * width)],
            held.at[p, :, pl.ds(q * width, size * width)],
            sems.at[p, q],
        )

    def move(loads):
        stores = [pltpu.make_async_copy(held.at[p], out_ref.at[p], out_sems.at[p]) for p in range(EIGHT)]
        for group in loads:
            for copy in group:
                copy.start()
        for group, store in zip(loads, stores):
            for copy in group:
                copy.wait()
            store.start()
        for store in stores:
            store.wait()

    @pl.when(core_ref[0] == 0)
    def _():
        move([[load(FOUR * p, FOUR, p, 0)] for p in range(EIGHT)])

    @pl.when(core_ref[0] != 0)
    def _():
        move([[load(EIGHT * q + p, 1, p, q) for q in range(FOUR)] for p in range(EIGHT)])


def split_columns(core, feats):
    tokens, width = feats.shape
    shape = (EIGHT, tokens, width // EIGHT)
    return pl.pallas_call(
        split_kernel,
        out_shape=jax.ShapeDtypeStruct(shape, feats.dtype),
        in_specs=[pl.BlockSpec(memory_space=pltpu.SMEM), pl.BlockSpec(memory_space=pltpu.HBM)],
        out_specs=pl.BlockSpec(memory_space=pltpu.HBM),
        scratch_shapes=[
            pltpu.VMEM(shape, feats.dtype),
            pltpu.SemaphoreType.DMA((EIGHT, FOUR)),
            pltpu.SemaphoreType.DMA((EIGHT,)),
        ],
        compiler_params=pltpu.CompilerParams(vmem_limit_bytes=60 * 1024 * 1024),
        cost_estimate=pl.CostEstimate(flops=0, bytes_accessed=4 * tokens * width, transcendentals=0),
    )(core, feats)


def gather_rows(x):
    out = [x]
    for step in range(1, FOUR):
        pairs = [(ring[i], ring[(i + step) % FOUR]) for ring in RINGS_OF_4 for i in range(FOUR)]
        out.append(lax.ppermute(x, ALL, pairs))
    return out


def exchange(x, rings):
    return lax.all_to_all(x, ALL, 0, 0, axis_index_groups=rings)


def gather_by_permutes(x, axis):
    size = lax.axis_size(axis)
    me = lax.axis_index(axis)
    out = jnp.zeros((size,) + x.shape, x.dtype)
    for step in range(size):
        piece = x
        if step:
            piece = lax.ppermute(x, axis, [(i, (i + step) % size) for i in range(size)])
        out = lax.dynamic_update_index_in_dim(out, piece, lax.rem(me + size - step, size), 0)
    return out


def project_kernel(q_ref, owned_ref, *refs):
    pieces, out_ref, weight_ref = refs[:-2], refs[-2], refs[-1]
    width = pieces[0].shape[0]
    for step, piece in enumerate(pieces):
        first = lax.rem(q_ref[0] + len(pieces) - step, len(pieces)) * width
        weight_ref[pl.ds(pl.multiple_of(first, width), width), :] = piece[...]
    block = owned_ref.shape[0] // 4
    for i in range(4):
        rows = slice(i * block, (i + 1) * block)
        out_ref[rows, :] = jnp.dot(
            owned_ref[rows, :], weight_ref[...], preferred_element_type=jnp.float32
        ).astype(out_ref.dtype)


def project(q, owned, pieces):
    rows, depth = owned.shape
    columns = pieces[0].shape[1]
    return pl.pallas_call(
        project_kernel,
        out_shape=jax.ShapeDtypeStruct((rows, columns), jnp.bfloat16),
        in_specs=[pl.BlockSpec(memory_space=pltpu.SMEM)]
        + [pl.BlockSpec(memory_space=pltpu.VMEM)] * (1 + len(pieces)),
        out_specs=pl.BlockSpec(memory_space=pltpu.VMEM),
        scratch_shapes=[pltpu.VMEM((depth, columns), jnp.bfloat16)],
        compiler_params=pltpu.CompilerParams(vmem_limit_bytes=12 * 1024 * 1024),
        cost_estimate=pl.CostEstimate(
            flops=2 * rows * depth * columns,
            bytes_accessed=2 * (rows * depth + depth * columns + rows * columns),
            transcendentals=0,
        ),
    )(q, owned, *pieces)


MARKS = 16


def gradient_kernel(owned_ref, slopes_ref, out_ref, all_slopes_ref):
    pieces, columns, tokens = slopes_ref.shape
    largest = jnp.abs(slopes_ref[0])
    for piece in range(pieces):
        all_slopes_ref[:, piece * tokens : (piece + 1) * tokens] = slopes_ref[piece]
        if piece:
            largest = jnp.maximum(largest, jnp.abs(slopes_ref[piece]))
    largest = jnp.max(largest.astype(jnp.float32), axis=0, keepdims=True)
    bound = 30.0 * owned_ref.shape[0] * jnp.max(largest, axis=1, keepdims=True)
    exponent = jnp.ceil(jnp.log2(jnp.maximum(bound, 1e-30))) - 15.0
    receivers, _, rows = out_ref.shape
    for i in range(receivers):
        sums = jnp.dot(
            all_slopes_ref[...],
            owned_ref[:, i * rows : (i + 1) * rows],
            preferred_element_type=jnp.float32,
        )
        out_ref[i, :columns] = sums * jnp.exp2(-exponent)
        out_ref[i, columns:] = jnp.broadcast_to(exponent, (MARKS, rows))


def gradient_parts(owned, slopes, receivers):
    tokens, width = owned.shape
    columns = slopes.shape[1]
    rows = width // receivers
    return pl.pallas_call(
        gradient_kernel,
        out_shape=jax.ShapeDtypeStruct((receivers, columns + MARKS, rows), jnp.float32),
        in_specs=[pl.BlockSpec(memory_space=pltpu.VMEM)] * 2,
        out_specs=pl.BlockSpec(memory_space=pltpu.VMEM),
        scratch_shapes=[pltpu.VMEM((columns, tokens), jnp.bfloat16)],
        compiler_params=pltpu.CompilerParams(vmem_limit_bytes=12 * 1024 * 1024),
        cost_estimate=pl.CostEstimate(
            flops=2 * tokens * width * columns,
            bytes_accessed=2 * (tokens * width + tokens * columns) + 4 * width * columns,
            transcendentals=0,
        ),
    )(owned, slopes)


def squares_kernel(gradient_ref, out_ref):
    gradient = gradient_ref[...]
    columns = jnp.sum(gradient * gradient, axis=0, keepdims=True)
    out_ref[...] = jnp.broadcast_to(jnp.sum(columns, axis=1, keepdims=True), out_ref.shape)


def squares_for_all(gradient, receivers):
    return pl.pallas_call(
        squares_kernel,
        out_shape=jax.ShapeDtypeStruct((receivers, 8, 128), jnp.float32),
        compiler_params=pltpu.CompilerParams(vmem_limit_bytes=8 * 1024 * 1024),
        cost_estimate=pl.CostEstimate(flops=2 * gradient.size, bytes_accessed=4 * gradient.size, transcendentals=0),
    )(gradient)


def step_kernel(size, shares_ref, own_ref, gradient_ref, after_ref):
    rate = inner_rate / jnp.sqrt(jnp.sum(shares_ref[...], axis=0) / size + epsilon)
    after_ref[...] = own_ref[...].T - rate[0:1, 0:1] * gradient_ref[...]


def step(shares, own_rows, gradient_t):
    size = shares.shape[0] * own_rows.size
    return pl.pallas_call(
        functools.partial(step_kernel, size),
        out_shape=jax.ShapeDtypeStruct(gradient_t.shape, jnp.float32),
        compiler_params=pltpu.CompilerParams(vmem_limit_bytes=8 * 1024 * 1024),
        cost_estimate=pl.CostEstimate(flops=2 * own_rows.size, bytes_accessed=12 * own_rows.size, transcendentals=0),
    )(shares, own_rows, gradient_t)


def blend_kernel(after_ref, new_ref, out_ref):
    cores, y_los, xs, width, _ = new_ref.shape
    size = 2 * cores * width
    for y_lo in range(y_los):
        for x in range(0, xs, 2):
            pieces = [new_ref[core, y_lo, x + i] for i in range(2) for core in range(cores)]
            first = (y_lo * xs + x) * cores * width
            part = slice(first, first + size)
            new = jnp.concatenate(pieces, axis=0)
            out_ref[:, part] = (blend_rate * new + (1.0 - blend_rate) * after_ref[part, :]).T


def blend(after_step_t, new_rows_t):
    return pl.pallas_call(
        blend_kernel,
        out_shape=jax.ShapeDtypeStruct(after_step_t.shape[::-1], jnp.float32),
        compiler_params=pltpu.CompilerParams(vmem_limit_bytes=8 * 1024 * 1024),
        cost_estimate=pl.CostEstimate(
            flops=3 * after_step_t.size, bytes_accessed=12 * after_step_t.size, transcendentals=0
        ),
    )(after_step_t, new_rows_t)


def shards(
    activations, key_cotangent, key_gain, local_weight, global_weight, outer_momentum, late_delta
):
    feats = activations[0]
    own_rows = local_weight[0]
    tokens, width = feats.shape
    rows, columns = own_rows.shape
    factor = width ** (-0.5)
    replicas = lax.axis_size(REPLICA)

    core = lax.axis_index("core")
    q = jnp.where(core == 0, lax.axis_index("y_hi"), lax.axis_index("z") // 2)

    owned = exchange(split_columns(core.reshape(1), feats), RINGS_OF_8)
    owned = owned.reshape(EIGHT * tokens, width // EIGHT)
    weight = gather_rows(own_rows.astype(jnp.bfloat16))

    global_t, momentum_t, late_t = global_weight.T, outer_momentum.T, late_delta.T
    next_momentum_t = keep_rate * momentum_t + late_t
    next_global_t = global_t - outer_rate * (late_t + keep_rate * next_momentum_t)
    new_rows_t = gather_by_permutes(gather_by_permutes(next_global_t, "x"), "y_lo")
    owned, weight, new_rows_t = lax.optimization_barrier((owned, weight, new_rows_t))
    parts = project(q.reshape(1), owned, weight).reshape(EIGHT, tokens, columns)
    parts = exchange(parts, RINGS_OF_8)
    slopes = key_slopes(parts, key_cotangent[0], key_gain.reshape(1, HEAD), factor)
    slopes, new_rows_t = lax.optimization_barrier((slopes, new_rows_t))
    new_rows_t = gather_by_permutes(new_rows_t, "core")
    slopes = exchange(slopes, RINGS_OF_8)
    slopes, new_rows_t = lax.optimization_barrier((slopes, new_rows_t))

    scaled = gradient_parts(owned, slopes, FOUR).astype(jnp.float16)
    pieces = exchange(scaled, RINGS_OF_4)
    unscale = jnp.exp2(pieces[:, columns, 0].astype(jnp.float32)) * factor
    gradient_t = jnp.sum(pieces[:, :columns].astype(jnp.float32) * unscale[:, None, None], axis=0)
    shares = lax.all_to_all(squares_for_all(gradient_t, EIGHT * FOUR), FSDP, 0, 0)
    after_step_t = step(shares, own_rows, gradient_t)

    sent_rows = after_step_t.reshape(replicas, columns // replicas, rows)
    received = lax.all_to_all(sent_rows.astype(jnp.float16), REPLICA, 0, 0).astype(jnp.float32)
    outer_delta_t = global_t - jnp.sum(received, axis=0) / replicas
    next_local = blend(after_step_t, new_rows_t)
    return (next_local[None], next_global_t.T, next_momentum_t.T, outer_delta_t.T)


def solution(mesh):
    split = Mesh(mesh.devices.reshape(2, 4, 2, 8, 4), ("y_lo", "x", "core", "z", "y_hi"))
    whole = P(REPLICA, FSDP, None)
    outer = P(FSDP, REPLICA)
    return jax.shard_map(
        shards,
        mesh=split,
        in_specs=(whole, whole, P(), whole, outer, outer, outer),
        out_specs=(whole, outer, outer, outer),
        check_vma=False,
    )
```

```python
import functools

import jax
import jax.numpy as jnp
from jax import lax
from jax.experimental import pallas as pl
from jax.experimental.pallas import tpu as pltpu
from jax.sharding import Mesh
from jax.sharding import PartitionSpec as P

HEAD = 128

inner_rate = 0.5
outer_rate = 0.7
keep_rate = 0.9
blend_rate = 0.5
epsilon = 1e-06

REPLICA = ("y_lo", "x", "core")
FSDP = ("z", "y_hi")
ALL = REPLICA + FSDP

EIGHT, FOUR = 8, 4


def place(core, p, q):
    return (p, q) if core == 0 else (2 * q + p // 4, p % 4)


def device(y_lo, x, core, p, q):
    z, y_hi = place(core, p, q)
    return (((y_lo * 4 + x) * 2 + core) * 8 + z) * 4 + y_hi


TEAMS = [(y_lo, x, core) for y_lo in range(2) for x in range(4) for core in range(2)]
RINGS_OF_8 = [[device(*team, p, q) for p in range(EIGHT)] for team in TEAMS for q in range(FOUR)]
RINGS_OF_4 = [[device(*team, p, q) for q in range(FOUR)] for team in TEAMS for p in range(EIGHT)]


def slope_kernel(factor, parts_ref, cotangent_ref, gain_ref, out_ref):
    pieces = parts_ref.shape[0]
    gain = gain_ref[...]
    for head in range(out_ref.shape[1] // HEAD):
        lanes = slice(head * HEAD, (head + 1) * HEAD)
        hidden = parts_ref[0, :, lanes].astype(jnp.float32)
        for piece in range(1, pieces):
            hidden = hidden + parts_ref[piece, :, lanes].astype(jnp.float32)
        hidden = hidden * factor
        spread = jnp.sqrt(jnp.mean(hidden * hidden, axis=-1, keepdims=True) + epsilon)
        unit = hidden / spread
        slope = cotangent_ref[:, lanes].astype(jnp.float32) * gain
        key_slope = (slope - unit * jnp.mean(slope * unit, axis=-1, keepdims=True)) / spread
        key_slope = key_slope.T.astype(jnp.bfloat16)
        for piece in range(out_ref.shape[0]):
            out_ref[piece, lanes, :] = key_slope


def key_slopes(parts, cotangent, gain, factor):
    return pl.pallas_call(
        functools.partial(slope_kernel, factor),
        out_shape=jax.ShapeDtypeStruct((parts.shape[0],) + parts.shape[:0:-1], jnp.bfloat16),
        compiler_params=pltpu.CompilerParams(vmem_limit_bytes=8 * 1024 * 1024),
        cost_estimate=pl.CostEstimate(flops=2_000_000, bytes_accessed=2_500_000, transcendentals=2000),
    )(parts, cotangent, gain)


def split_kernel(core_ref, feats_ref, out_ref, held, sems, out_sems):
    width = feats_ref.shape[1] // (EIGHT * FOUR)

    def load(first, size, p, q):
        return pltpu.make_async_copy(
            feats_ref.at[:, pl.ds(first * width, size * width)],
            held.at[p, :, pl.ds(q * width, size * width)],
            sems.at[p, q],
        )

    def move(loads):
        stores = [pltpu.make_async_copy(held.at[p], out_ref.at[p], out_sems.at[p]) for p in range(EIGHT)]
        for group in loads:
            for copy in group:
                copy.start()
        for group, store in zip(loads, stores):
            for copy in group:
                copy.wait()
            store.start()
        for store in stores:
            store.wait()

    @pl.when(core_ref[0] == 0)
    def _():
        move([[load(FOUR * p, FOUR, p, 0)] for p in range(EIGHT)])

    @pl.when(core_ref[0] != 0)
    def _():
        move([[load(EIGHT * q + p, 1, p, q) for q in range(FOUR)] for p in range(EIGHT)])


def split_columns(core, feats):
    tokens, width = feats.shape
    shape = (EIGHT, tokens, width // EIGHT)
    return pl.pallas_call(
        split_kernel,
        out_shape=jax.ShapeDtypeStruct(shape, feats.dtype),
        in_specs=[pl.BlockSpec(memory_space=pltpu.SMEM), pl.BlockSpec(memory_space=pltpu.HBM)],
        out_specs=pl.BlockSpec(memory_space=pltpu.HBM),
        scratch_shapes=[
            pltpu.VMEM(shape, feats.dtype),
            pltpu.SemaphoreType.DMA((EIGHT, FOUR)),
            pltpu.SemaphoreType.DMA((EIGHT,)),
        ],
        compiler_params=pltpu.CompilerParams(vmem_limit_bytes=60 * 1024 * 1024),
        cost_estimate=pl.CostEstimate(flops=0, bytes_accessed=4 * tokens * width, transcendentals=0),
    )(core, feats)


def gather_rows(x):
    out = [x]
    for step in range(1, FOUR):
        pairs = [(ring[i], ring[(i + step) % FOUR]) for ring in RINGS_OF_4 for i in range(FOUR)]
        out.append(lax.ppermute(x, ALL, pairs))
    return out


def exchange(x, rings):
    return lax.all_to_all(x, ALL, 0, 0, axis_index_groups=rings)


def gather_by_permutes(x, axis):
    size = lax.axis_size(axis)
    me = lax.axis_index(axis)
    out = jnp.zeros((size,) + x.shape, x.dtype)
    for step in range(size):
        piece = x
        if step:
            piece = lax.ppermute(x, axis, [(i, (i + step) % size) for i in range(size)])
        out = lax.dynamic_update_index_in_dim(out, piece, lax.rem(me + size - step, size), 0)
    return out


def project_kernel(q_ref, owned_ref, *refs):
    pieces, out_ref, weight_ref = refs[:-2], refs[-2], refs[-1]
    width = pieces[0].shape[0]
    for step, piece in enumerate(pieces):
        first = lax.rem(q_ref[0] + len(pieces) - step, len(pieces)) * width
        weight_ref[pl.ds(pl.multiple_of(first, width), width), :] = piece[...]
    block = owned_ref.shape[0] // 4
    for i in range(4):
        rows = slice(i * block, (i + 1) * block)
        out_ref[rows, :] = jnp.dot(
            owned_ref[rows, :], weight_ref[...], preferred_element_type=jnp.float32
        ).astype(out_ref.dtype)


def project(q, owned, pieces):
    rows, depth = owned.shape
    columns = pieces[0].shape[1]
    return pl.pallas_call(
        project_kernel,
        out_shape=jax.ShapeDtypeStruct((rows, columns), jnp.bfloat16),
        in_specs=[pl.BlockSpec(memory_space=pltpu.SMEM)]
        + [pl.BlockSpec(memory_space=pltpu.VMEM)] * (1 + len(pieces)),
        out_specs=pl.BlockSpec(memory_space=pltpu.VMEM),
        scratch_shapes=[pltpu.VMEM((depth, columns), jnp.bfloat16)],
        compiler_params=pltpu.CompilerParams(vmem_limit_bytes=12 * 1024 * 1024),
        cost_estimate=pl.CostEstimate(
            flops=2 * rows * depth * columns,
            bytes_accessed=2 * (rows * depth + depth * columns + rows * columns),
            transcendentals=0,
        ),
    )(q, owned, *pieces)


MARKS = 16


def gradient_kernel(owned_ref, slopes_ref, out_ref, all_slopes_ref):
    pieces, columns, tokens = slopes_ref.shape
    largest = jnp.abs(slopes_ref[0])
    for piece in range(pieces):
        all_slopes_ref[:, piece * tokens : (piece + 1) * tokens] = slopes_ref[piece]
        if piece:
            largest = jnp.maximum(largest, jnp.abs(slopes_ref[piece]))
    largest = jnp.max(largest.astype(jnp.float32), axis=0, keepdims=True)
    bound = 30.0 * owned_ref.shape[0] * jnp.max(largest, axis=1, keepdims=True)
    exponent = jnp.ceil(jnp.log2(jnp.maximum(bound, 1e-30))) - 15.0
    receivers, _, rows = out_ref.shape
    for i in range(receivers):
        sums = jnp.dot(
            all_slopes_ref[...],
            owned_ref[:, i * rows : (i + 1) * rows],
            preferred_element_type=jnp.float32,
        )
        out_ref[i, :columns] = sums * jnp.exp2(-exponent)
        out_ref[i, columns:] = jnp.broadcast_to(exponent, (MARKS, rows))


def gradient_parts(owned, slopes, receivers):
    tokens, width = owned.shape
    columns = slopes.shape[1]
    rows = width // receivers
    return pl.pallas_call(
        gradient_kernel,
        out_shape=jax.ShapeDtypeStruct((receivers, columns + MARKS, rows), jnp.float32),
        in_specs=[pl.BlockSpec(memory_space=pltpu.VMEM)] * 2,
        out_specs=pl.BlockSpec(memory_space=pltpu.VMEM),
        scratch_shapes=[pltpu.VMEM((columns, tokens), jnp.bfloat16)],
        compiler_params=pltpu.CompilerParams(vmem_limit_bytes=12 * 1024 * 1024),
        cost_estimate=pl.CostEstimate(
            flops=2 * tokens * width * columns,
            bytes_accessed=2 * (tokens * width + tokens * columns) + 4 * width * columns,
            transcendentals=0,
        ),
    )(owned, slopes)


def squares_kernel(gradient_ref, out_ref):
    gradient = gradient_ref[...]
    columns = jnp.sum(gradient * gradient, axis=0, keepdims=True)
    out_ref[...] = jnp.broadcast_to(jnp.sum(columns, axis=1, keepdims=True), out_ref.shape)


def squares_for_all(gradient, receivers):
    return pl.pallas_call(
        squares_kernel,
        out_shape=jax.ShapeDtypeStruct((receivers, 8, 128), jnp.float32),
        compiler_params=pltpu.CompilerParams(vmem_limit_bytes=8 * 1024 * 1024),
        cost_estimate=pl.CostEstimate(flops=2 * gradient.size, bytes_accessed=4 * gradient.size, transcendentals=0),
    )(gradient)


def step_kernel(size, shares_ref, own_ref, gradient_ref, after_ref):
    rate = inner_rate / jnp.sqrt(jnp.sum(shares_ref[...], axis=0) / size + epsilon)
    after_ref[...] = own_ref[...].T - rate[0:1, 0:1] * gradient_ref[...]


def step(shares, own_rows, gradient_t):
    size = shares.shape[0] * own_rows.size
    return pl.pallas_call(
        functools.partial(step_kernel, size),
        out_shape=jax.ShapeDtypeStruct(gradient_t.shape, jnp.float32),
        compiler_params=pltpu.CompilerParams(vmem_limit_bytes=8 * 1024 * 1024),
        cost_estimate=pl.CostEstimate(flops=2 * own_rows.size, bytes_accessed=12 * own_rows.size, transcendentals=0),
    )(shares, own_rows, gradient_t)


def blend_kernel(after_ref, new_ref, out_ref):
    cores, y_los, xs, width, _ = new_ref.shape
    size = 2 * cores * width
    for y_lo in range(y_los):
        for x in range(0, xs, 2):
            pieces = [new_ref[core, y_lo, x + i] for i in range(2) for core in range(cores)]
            first = (y_lo * xs + x) * cores * width
            part = slice(first, first + size)
            new = jnp.concatenate(pieces, axis=0)
            out_ref[:, part] = (blend_rate * new + (1.0 - blend_rate) * after_ref[part, :]).T


def blend(after_step_t, new_rows_t):
    return pl.pallas_call(
        blend_kernel,
        out_shape=jax.ShapeDtypeStruct(after_step_t.shape[::-1], jnp.float32),
        compiler_params=pltpu.CompilerParams(vmem_limit_bytes=8 * 1024 * 1024),
        cost_estimate=pl.CostEstimate(
            flops=3 * after_step_t.size, bytes_accessed=12 * after_step_t.size, transcendentals=0
        ),
    )(after_step_t, new_rows_t)


def shards(
    activations, key_cotangent, key_gain, local_weight, global_weight, outer_momentum, late_delta
):
    feats = activations[0]
    own_rows = local_weight[0]
    tokens, width = feats.shape
    rows, columns = own_rows.shape
    factor = width ** (-0.5)
    replicas = lax.axis_size(REPLICA)

    core = lax.axis_index("core")
    q = jnp.where(core == 0, lax.axis_index("y_hi"), lax.axis_index("z") // 2)

    owned = exchange(split_columns(core.reshape(1), feats), RINGS_OF_8)
    owned = owned.reshape(EIGHT * tokens, width // EIGHT)
    weight = gather_rows(own_rows.astype(jnp.bfloat16))

    global_t, momentum_t, late_t = global_weight.T, outer_momentum.T, late_delta.T
    next_momentum_t = keep_rate * momentum_t + late_t
    next_global_t = global_t - outer_rate * (late_t + keep_rate * next_momentum_t)
    new_rows_t = next_global_t.astype(jnp.float16)
    new_rows_t = gather_by_permutes(gather_by_permutes(new_rows_t, "x"), "y_lo")
    owned, weight, new_rows_t = lax.optimization_barrier((owned, weight, new_rows_t))
    parts = project(q.reshape(1), owned, weight).reshape(EIGHT, tokens, columns)
    parts = exchange(parts, RINGS_OF_8)
    slopes = key_slopes(parts, key_cotangent[0], key_gain.reshape(1, HEAD), factor)
    slopes, new_rows_t = lax.optimization_barrier((slopes, new_rows_t))
    new_rows_t = gather_by_permutes(new_rows_t, "core")
    slopes = exchange(slopes, RINGS_OF_8)
    slopes, new_rows_t = lax.optimization_barrier((slopes, new_rows_t))

    scaled = gradient_parts(owned, slopes, FOUR).astype(jnp.float16)
    pieces = exchange(scaled, RINGS_OF_4)
    unscale = jnp.exp2(pieces[:, columns, 0].astype(jnp.float32)) * factor
    gradient_t = jnp.sum(pieces[:, :columns].astype(jnp.float32) * unscale[:, None, None], axis=0)
    shares = lax.all_to_all(squares_for_all(gradient_t, EIGHT * FOUR), FSDP, 0, 0)
    after_step_t = step(shares, own_rows, gradient_t)

    sent_rows = after_step_t.reshape(replicas, columns // replicas, rows)
    received = lax.all_to_all(sent_rows.astype(jnp.float16), REPLICA, 0, 0).astype(jnp.float32)
    outer_delta_t = global_t - jnp.sum(received, axis=0) / replicas
    next_local = blend(after_step_t, new_rows_t.astype(jnp.float32))
    return (next_local[None], next_global_t.T, next_momentum_t.T, outer_delta_t.T)


def solution(mesh):
    split = Mesh(mesh.devices.reshape(2, 4, 2, 8, 4), ("y_lo", "x", "core", "z", "y_hi"))
    whole = P(REPLICA, FSDP, None)
    outer = P(FSDP, REPLICA)
    return jax.shard_map(
        shards,
        mesh=split,
        in_specs=(whole, whole, P(), whole, outer, outer, outer),
        out_specs=(whole, outer, outer, outer),
        check_vma=False,
    )
```
